512 devices in a mesh: tube: 16 (over z), lon: 32 (over y, x, core).
Axes of the slice: x: 4, y: 4, z: 16, core: 2. Of those that a mesh axis runs over, the one named last changes fastest.
Arguments:
- density: float32 [7, 512, 256, 128], P(None, 'tube', 'lon'), may hold values from 0.5 to 5
- pedersen: float32 [512, 256, 128], P('tube', 'lon'), may hold values from 0.1 to 10
- neutral_wind: float32 [512, 256, 128], P('tube', 'lon'), may hold values from -6 to 6
- along_courant: float32 [7, 512], P(None, 'tube'), may hold values from 0.45 to 20000
Outputs:
- density_next: float32 [7, 512, 256, 128], P(None, 'tube', 'lon')
- potential: float32 [256, 128], P('lon')
The draws below stay inside these ranges and needn't reach their ends.
All inputs are finite; a program needn't handle non-finite values.
Results may differ from the reference program's by a relative error of at most 0.00016.
Values sent between devices are 32-bit elements; how exact they have to be, the bound alone decides.
A program may use at most 64 MiB of HBM per device.

```python
import math
import jax
import jax.numpy as jnp
from jax import lax

ION_SPECIES = 7
LAT = 128
LEVELS = 3
CYCLES = 3
LINE_POINTS = 512
LON = 256


def draw_along_courant(key, part):
    first, second, third_part = jax.random.split(jax.random.fold_in(key, 17), 3)
    base = jax.random.uniform(first, (ION_SPECIES, 1), jnp.float32, 0.0, 9.9)
    rough = 0.5 * jax.random.normal(second, (ION_SPECIES, LINE_POINTS), jnp.float32)
    logarithm_rate = jnp.clip(base + rough, -0.7, 9.9)
    source_pulses = jax.random.randint(third_part, (ION_SPECIES, LINE_POINTS), 0, LINE_POINTS) < 3
    return jnp.where(source_pulses, 1.0, jnp.exp(logarithm_rate)).astype(jnp.float32)


def draw_pedersen(key, part):
    lon_key, lat_key, rough_key = jax.random.split(jax.random.fold_in(key, 29), 3)
    lon_levels = jax.random.uniform(lon_key, (16,), jnp.float32, -1.6, 1.6)
    lat_levels = jax.random.uniform(lat_key, (8,), jnp.float32, -1.6, 1.6)
    lon_block = (jnp.arange(LON) * 16 // LON).astype(jnp.int32)
    lat_block = (jnp.arange(LAT) * 8 // LAT).astype(jnp.int32)
    level = lon_levels[lon_block][:, None] + lat_levels[lat_block][None, :]
    rough = jnp.clip(0.35 * jax.random.normal(rough_key, (LINE_POINTS, LON, LAT), jnp.float32), -0.7, 0.7)
    return jnp.clip(jnp.exp(level[None, :, :] + rough), 0.1, 10.0).astype(jnp.float32)


def levels(rng, shape, pieces, least, largest):
    level, own = 1.0, jax.random.fold_in(rng, 6)
    for axis_at, blocks in pieces:
        draws = jnp.exp(jax.random.uniform(jax.random.fold_in(own, axis_at), (blocks,), jnp.float32, least / len(pieces), largest / len(pieces)))
        level = level * jnp.repeat(draws, shape[axis_at] // blocks).reshape([-1 if axis == axis_at else 1 for axis in range(len(shape))])
    return level


def scatter_about(rng, dims, width, reach, cuts=(), held_as=jnp.bfloat16):
    loudness = levels(rng, dims, cuts, -0.22, 0.18) if cuts else 1.0
    drawn = jax.random.normal(rng, dims, jnp.float32) * width * loudness
    return jnp.minimum(jnp.maximum(drawn, -reach), reach).astype(held_as)


def setup_inputs(seed: int = 0) -> dict:
    key_list = jax.random.split(jax.random.key(seed), 5)
    density = jnp.clip(jnp.exp(math.log(5.0) - 2.3025851 * jax.random.uniform(key_list[0], (ION_SPECIES, LINE_POINTS, LON, LAT), jnp.float32) ** levels(key_list[0], (ION_SPECIES, LINE_POINTS, LON, LAT), ((1, 16), (2, 32)), -0.2, 0.2)), 0.5, 5.0)
    pedersen = draw_pedersen(jax.random.fold_in(key_list[4], 71), 0)
    neutral_wind = scatter_about(key_list[2], (LINE_POINTS, LON, LAT), 1.0, 6.0, ((0, 16), (1, 32)), jnp.float32)
    along_courant = draw_along_courant(jax.random.fold_in(key_list[4], 71), 0)
    return {"density": density, "pedersen": pedersen, "neutral_wind": neutral_wind, "along_courant": along_courant}


SCREENING = 0.005
RELAXATION = 0.8
DRIFT_GAIN = 1.0
COURANT_CAP = 0.2

def lat_zeros(periodic_copy):
    return jnp.pad(periodic_copy, ((0, 0), (1, 1)))

def grid_pad(grid_field):
    periodic_copy = jnp.concatenate([grid_field[-1:], grid_field, grid_field[:1]], axis=0)
    return lat_zeros(periodic_copy)

def face_weights(cond_pad):
    middle = cond_pad[1:-1, 1:-1]
    return (0.5 * (cond_pad[:-2, 1:-1] + middle), 0.5 * (cond_pad[2:, 1:-1] + middle), 0.5 * (cond_pad[1:-1, :-2] + middle), 0.5 * (cond_pad[1:-1, 2:] + middle))

def apply_operator(field_pad, weights, level_scale):
    middle = field_pad[1:-1, 1:-1]
    net_flux = weights[0] * (middle - field_pad[:-2, 1:-1]) + weights[1] * (middle - field_pad[2:, 1:-1])
    net_flux = net_flux + weights[2] * (middle - field_pad[1:-1, :-2]) + weights[3] * (middle - field_pad[1:-1, 2:])
    return level_scale * net_flux + SCREENING * middle

def diagonal_of(weights, level_scale):
    return level_scale * (weights[0] + weights[1] + weights[2] + weights[3]) + SCREENING

def coarsen(grid_field):
    return 0.25 * grid_field.reshape(grid_field.shape[0] // 2, 2, grid_field.shape[1] // 2, 2).sum(axis=(1, 3))

def refine(grid_field):
    return jnp.repeat(jnp.repeat(grid_field, 2, axis=0), 2, axis=1)

def dense_operator(grid_cond, level_scale):
    unknowns = grid_cond.shape[0] * grid_cond.shape[1]
    weights = face_weights(grid_pad(grid_cond))
    unit_fields = jnp.eye(unknowns, dtype=jnp.float32).reshape(unknowns, grid_cond.shape[0], grid_cond.shape[1])
    matrix_rows = jax.vmap(lambda unit_field: apply_operator(grid_pad(unit_field), weights, level_scale))(unit_fields)
    return matrix_rows.reshape(unknowns, unknowns)

def vcycle(level_index, right_side, start_field, weights, diagonals, padder, coarse_solve):
    if level_index == len(weights):
        return coarse_solve(right_side)
    level_scale = 0.25 ** level_index
    if start_field is None:
        relaxed_potential = RELAXATION * right_side / diagonals[level_index]
    else:
        relaxed_potential = start_field + RELAXATION * (right_side - apply_operator(padder(start_field), weights[level_index], level_scale)) / diagonals[level_index]
    residual = right_side - apply_operator(padder(relaxed_potential), weights[level_index], level_scale)
    relaxed_potential = relaxed_potential + refine(vcycle(level_index + 1, coarsen(residual), None, weights, diagonals, padder, coarse_solve))
    return relaxed_potential + RELAXATION * (right_side - apply_operator(padder(relaxed_potential), weights[level_index], level_scale)) / diagonals[level_index]

def drifts(padded):
    lon_drift = COURANT_CAP * jnp.tanh(-DRIFT_GAIN * 0.25 * (padded[:-1, 2:] + padded[1:, 2:] - (padded[:-1, :-2] + padded[1:, :-2])))
    lat_raw = DRIFT_GAIN * 0.25 * (padded[2:, :-1] + padded[2:, 1:] - (padded[:-2, :-1] + padded[:-2, 1:]))
    column = jnp.arange(lat_raw.shape[1])
    inside = (column > 0) & (column < lat_raw.shape[1] - 1)
    lat_drift = jnp.where(inside[None, :], COURANT_CAP * jnp.tanh(lat_raw), 0.0)
    return (lon_drift, lat_drift)

def transport(rimmed, lon_drift, lat_drift):
    interior = rimmed[:, :, 1:-1]
    east_flux = jnp.maximum(lon_drift, 0.0) * rimmed[:, :, :-1] + jnp.minimum(lon_drift, 0.0) * rimmed[:, :, 1:]
    lat_padded = jnp.pad(interior, ((0, 0), (0, 0), (0, 0), (1, 1)))
    north_flux = jnp.maximum(lat_drift, 0.0) * lat_padded[..., :-1] + jnp.minimum(lat_drift, 0.0) * lat_padded[..., 1:]
    return interior - (east_flux[:, :, 1:] - east_flux[:, :, :-1]) - (north_flux[..., 1:] - north_flux[..., :-1])

def reference(density, pedersen, neutral_wind, along_courant):
    conductance = jnp.sum(pedersen, axis=0) / LINE_POINTS
    source = jnp.sum(pedersen * neutral_wind, axis=0) / LINE_POINTS
    conductances = [conductance]
    for level_index in range(LEVELS):
        conductances.append(coarsen(conductances[-1]))
    weights = [face_weights(grid_pad(conductances[level_index])) for level_index in range(LEVELS)]
    diagonals = [diagonal_of(weights[level_index], 0.25 ** level_index) for level_index in range(LEVELS)]
    factor = jnp.linalg.cholesky(dense_operator(conductances[LEVELS], 0.25 ** LEVELS))

    def coarse_solve(right_side):
        return jax.scipy.linalg.cho_solve((factor, True), right_side.reshape(-1)).reshape(right_side.shape)
    potential = None
    for sweep_index in range(CYCLES):
        potential = vcycle(0, source, potential, weights, diagonals, grid_pad, coarse_solve)
    keep_rate = along_courant / (1.0 + along_courant)
    inflow = density / (1.0 + along_courant)[:, :, None, None]

    def advance(carried, inputs_now):
        retain, arriving = inputs_now
        carried = retain[:, None, None] * carried + arriving
        return (carried, carried)
    initial = jnp.zeros((density.shape[0], density.shape[2], density.shape[3]), jnp.float32)
    _, aligned = lax.scan(advance, initial, (jnp.moveaxis(keep_rate, 1, 0), jnp.moveaxis(inflow, 1, 0)))
    aligned = jnp.moveaxis(aligned, 0, 1)
    rimmed = jnp.concatenate([aligned[:, :, -1:], aligned, aligned[:, :, :1]], axis=2)
    lon_drift, lat_drift = drifts(grid_pad(potential))
    return (transport(rimmed, lon_drift, lat_drift), potential)
```

```python
import functools

import jax
import jax.numpy as jnp
from jax import lax
from jax.experimental import pallas as pl
from jax.experimental.pallas import tpu as pltpu
from jax.sharding import PartitionSpec as P

F32 = jnp.float32
SCREENING = 0.005
CAP = 0.2
NV = 32
CYCLES = 3
MESH = pl.DeviceIdType.MESH


def exchange_kernel(
    nt, nl, ped, wind, cour, dens, gath, halo, ent, ent_l, ent_r,
    part, recv1, row, recv2, dloc, atab, btab, bsend, brecv, psend,
    s_ld, s_rs, r_rs, s_ag, r_ag, s_lg, r_lg, s_h, r_h, s_b, r_b, s_p, r_p, s_e, r_e,
):
    ns, pts = dens.shape[0], dens.shape[1]
    rp = 16 // nt
    t, l = lax.axis_index("tube"), lax.axis_index("lon")

    load = pltpu.make_async_copy(dens, dloc, s_ld)
    load.start()

    barrier = pltpu.get_barrier_semaphore()
    for o in range(1, nt):
        pl.semaphore_signal(
            barrier, inc=1, device_id=(lax.rem(t + o, nt), l), device_id_type=MESH
        )
    for o in range(1, nl):
        pl.semaphore_signal(
            barrier, inc=1, device_id=(t, lax.rem(l + o, nl)), device_id_type=MESH
        )

    csum = [ped[k] for k in range(4)]
    ssum = [ped[k] * wind[k] for k in range(4)]
    for p in range(4, pts):
        csum[p % 4] = csum[p % 4] + ped[p]
        ssum[p % 4] = ssum[p % 4] + ped[p] * wind[p]
    csum = (csum[0] + csum[1]) + (csum[2] + csum[3])
    ssum = (ssum[0] + ssum[1]) + (ssum[2] + ssum[3])
    for r in range(8):
        part[r // rp, r % rp, :] = csum[r]
        part[(8 + r) // rp, r % rp, :] = ssum[r]

    pl.semaphore_wait(barrier, nt + nl - 2)

    def remote(src, dst, ssem, rsem, to):
        c = pltpu.make_async_remote_copy(
            src_ref=src, dst_ref=dst, send_sem=ssem, recv_sem=rsem,
            device_id=to, device_id_type=MESH,
        )
        c.start()
        return c

    rs = []
    for o in range(1, nt):
        to = lax.rem(t + o, nt)
        rs.append(remote(part.at[to], recv1.at[o], s_rs.at[o], r_rs.at[o], (to, l)))
    recv1[0] = part[t]

    right, left = lax.rem(l + 1, nl), lax.rem(l + nl - 1, nl)
    h0 = remote(
        dens.at[:, :, pl.ds(7, 1), :], halo.at[:, :, pl.ds(0, 1), :], s_h.at[0], r_h.at[0], (t, right)
    )
    h1 = remote(
        dens.at[:, :, pl.ds(0, 1), :], halo.at[:, :, pl.ds(7, 1), :], s_h.at[1], r_h.at[1], (t, left)
    )

    coefficient_tables(cour, atab, btab)
    load.wait()

    def step(p, carry):
        out = []
        for s in range(ns):
            x, m = carry[s]
            a, b = row_of(atab, p * 8 + s), row_of(btab, p * 8 + s)
            out.append((a * x + b * dloc[s, p], a * m))
        return tuple(out)

    zero, one = jnp.zeros((8, 128), F32), jnp.ones((8, 128), F32)
    ends = lax.fori_loop(0, pts, step, tuple((zero, one) for _ in range(ns)))
    for s in range(ns):
        bsend[s, 0] = ends[s][0]
        bsend[s, 1] = ends[s][1]

    for c in rs:
        c.wait_recv()
    total = recv1[0]
    for o in range(1, nt):
        total = total + recv1[o]
    row[...] = total
    ag = []
    for o in range(1, nt):
        to = lax.rem(t + o, nt)
        ag.append(remote(row, recv2.at[t], s_ag.at[o], r_ag.at[o], (to, l)))
    recv2[t] = total

    mine = (t * ns + nt - 1) // nt
    owner_of = [(s * nt) // ns for s in range(ns)]
    is_owner = jnp.logical_and(mine < ns, (mine * nt) // ns == t)
    for s in range(ns):

        @pl.when(t != owner_of[s])
        def _():
            o = lax.rem(t - owner_of[s] + nt, nt)
            remote(bsend.at[s], brecv.at[o], s_b.at[s], r_b.at[o], (owner_of[s], l))

    for c in ag:
        c.wait_recv()
    own = pltpu.make_async_copy(recv2, gath.at[l], s_lg.at[0])
    own.start()
    lg = []
    for o in range(1, nl):
        to = lax.rem(l + o, nl)
        lg.append(remote(recv2, gath.at[l], s_lg.at[o], r_lg.at[o], (t, to)))

    @pl.when(is_owner)
    def _():
        brecv[0] = bsend[mine]
        for o in range(1, nt):
            pltpu.make_async_copy(brecv.at[o], brecv.at[o], r_b.at[o]).wait()
        x = zero
        for k in range(nt):
            psend[k] = x
            o = lax.rem(k - t + nt, nt)
            x = brecv[o, 1] * x + brecv[o, 0]
        ent[mine] = psend[t]
        for o in range(1, nt):
            to = lax.rem(t + o, nt)
            remote(psend.at[to], ent.at[mine], s_p.at[o], r_p.at[mine], (to, l))

    for s in range(ns):

        @pl.when(t != owner_of[s])
        def _():
            pltpu.make_async_copy(ent.at[s], ent.at[s], r_p.at[s]).wait()

    e0 = remote(ent, ent_l, s_e.at[0], r_e.at[0], (t, right))
    e1 = remote(ent, ent_r, s_e.at[1], r_e.at[1], (t, left))

    own.wait()
    for c in rs + ag + lg:
        c.wait_send()
    for c in lg:
        c.wait_recv()
    for s in range(ns):

        @pl.when(t != owner_of[s])
        def _():
            pltpu.make_async_copy(bsend.at[s], bsend.at[s], s_b.at[s]).wait()

    @pl.when(is_owner)
    def _():
        for o in range(1, nt):
            pltpu.make_async_copy(psend.at[0], psend.at[0], s_p.at[o]).wait()

    for c in (h0, h1, e0, e1):
        c.wait()


def exchange(mesh, density, pedersen, wind, courant):
    nt, nl = mesh.shape["tube"], mesh.shape["lon"]
    ns, pts = density.shape[:2]
    rp = 16 // nt
    vm = pl.BlockSpec(memory_space=pltpu.VMEM)
    hbm = pl.BlockSpec(memory_space=pl.ANY)
    dma = pltpu.SemaphoreType.DMA
    state = jax.ShapeDtypeStruct((ns, 8, 128), F32)
    return pl.pallas_call(
        functools.partial(exchange_kernel, nt, nl),
        out_shape=(
            jax.ShapeDtypeStruct((nl, nt, rp, 128), F32),
            jax.ShapeDtypeStruct(density.shape, F32),
            state, state, state,
        ),
        in_specs=[vm, vm, vm, hbm],
        out_specs=(vm, hbm, vm, vm, vm),
        scratch_shapes=[
            pltpu.VMEM((nt, rp, 128), F32),
            pltpu.VMEM((nt, rp, 128), F32),
            pltpu.VMEM((rp, 128), F32),
            pltpu.VMEM((nt, rp, 128), F32),
            pltpu.VMEM(density.shape, F32),
            pltpu.VMEM((pts * 8, 128), F32),
            pltpu.VMEM((pts * 8, 128), F32),
            pltpu.VMEM((ns, 2, 8, 128), F32),
            pltpu.VMEM((nt, 2, 8, 128), F32),
            pltpu.VMEM((nt, 8, 128), F32),
            dma,
            dma((nt,)), dma((nt,)), dma((nt,)), dma((nt,)),
            dma((nl,)), dma((nl,)),
            dma((2,)), dma((2,)),
            dma((ns,)), dma((nt,)),
            dma((nt,)), dma((ns,)),
            dma((2,)), dma((2,)),
        ],
        compiler_params=pltpu.CompilerParams(
            collective_id=0, has_side_effects=True, vmem_limit_bytes=40 * 2**20
        ),
        name="exchange",
    )(pedersen, wind, courant, density)


def row_of(ref, r):
    return jnp.broadcast_to(ref[pl.ds(r, 1), :], (8, 128))


def coefficient_tables(cour, atab, btab):
    c = cour[...]
    inv = 1.0 / (1.0 + c)
    keep = c * inv
    ns, pts = c.shape
    for p in range(pts):
        atab[pl.ds(p * 8, ns), :] = jnp.broadcast_to(keep[:, p : p + 1], (ns, 128))
        btab[pl.ds(p * 8, ns), :] = jnp.broadcast_to(inv[:, p : p + 1], (ns, 128))


def lroll(x, shift):
    return pltpu.roll(x, shift % 128, x.ndim - 1)


def before(x):
    return [pltpu.roll(x[-1], 1, 0)] + x[:-1]


def after(x):
    return x[1:] + [pltpu.roll(x[0], 7, 0)]


def level_weights(cond, level, wl, ws, wn, kk, dd):
    half, step, n = 0.5 * 0.25**level, 2**level, len(cond)
    lane = lax.broadcasted_iota(jnp.int32, (8, 128), 1)
    lo, hi = lane >= step, lane < 128 - step
    west = [half * (a + b) for a, b in zip(before(cond), cond)]
    west.append(pltpu.roll(west[0], 7, 0))
    for v in range(n + 1):
        wl[v] = west[v]
    for v in range(n):
        c = cond[v]
        south = half * (c + jnp.where(lo, lroll(c, step), 0.0))
        north = half * (c + jnp.where(hi, lroll(c, -step), 0.0))
        ws[v] = jnp.where(lo, south, 0.0)
        wn[v] = jnp.where(hi, north, 0.0)
        diagonal = (west[v] + west[v + 1]) + (south + north) + SCREENING
        kk[v] = 0.8 / diagonal
        if dd is not None:
            dd[v] = diagonal


def coarsened(x, step):
    lane = lax.broadcasted_iota(jnp.int32, (8, 128), 1)
    low = (lane // step) % 2 == 0
    out = []
    for v in range(0, len(x), 2):
        y = x[v] + x[v + 1]
        out.append(0.25 * (y + jnp.where(low, lroll(y, -step), lroll(y, step))))
    return out


def pulled(x, w, level):
    wl, ws, wn = w[:3]
    step, b, a = 2**level, before(x), after(x)
    return [
        (wl[v] * b[v] + wl[v + 1] * a[v])
        + (ws[v] * lroll(x[v], step) + wn[v] * lroll(x[v], -step))
        for v in range(len(x))
    ]


def vcycle(level, rhs, start, w, coarse):
    if level == len(w):
        return coarse(rhs)
    n = len(rhs)
    kk = w[level][3]
    if start is None:
        x = [kk[v] * rhs[v] for v in range(n)]
        e = [0.2 * r + p for r, p in zip(rhs, pulled(x, w[level], level))]
    else:
        dd = w[level][4]
        p = pulled(start, w[level], level)
        x = [0.2 * start[v] + kk[v] * (rhs[v] + p[v]) for v in range(n)]
        p = pulled(x, w[level], level)
        e = [(rhs[v] - dd[v] * x[v]) + p[v] for v in range(n)]
    fix = vcycle(level + 1, coarsened(e, 2**level), None, w, coarse)
    x = [x[v] + fix[v // 2] for v in range(n)]
    p = pulled(x, w[level], level)
    return [0.2 * x[v] + kk[v] * (rhs[v] + p[v]) for v in range(n)]


def to_ring(x, sq, sq2):
    for v in range(4):
        for rep in range(4):
            sq[pl.ds(rep * 32 + v, 8, stride=4), :] = x[v]
    sq2[...] = sq[...].T
    return [sq2[pl.ds(0, 8, stride=8), :], sq2[pl.ds(64, 8, stride=8), :]]


def from_ring(x, sq, sq2, vec):
    vec[pl.ds(0, 8), :], vec[pl.ds(8, 8), :] = x[0], x[1]
    for j in range(16):
        sq[pl.ds(j * 8, 8), :] = row_of(vec, j)
    sq2[...] = sq[...].T
    return [sq2[pl.ds(v, 8, stride=4), :] for v in range(4)]


def ring_matrix(c, bmat, emat):
    sub = [lax.broadcasted_iota(jnp.int32, (8, 128), 0) + 8 * h for h in range(2)]
    half = 0.5 * 0.25**3
    east = [half * (c[h] + lroll(c[h], -1)) for h in range(2)]
    up = [pltpu.roll(c[h], 1, 0) for h in range(2)]
    dn = [pltpu.roll(c[h], 7, 0) for h in range(2)]
    first, last = sub[0] % 8 == 0, sub[0] % 8 == 7
    below = [jnp.where(first, 0.0, up[0]), jnp.where(first, up[0], up[1])]
    above = [jnp.where(last, dn[1], dn[0]), jnp.where(last, 0.0, dn[1])]
    south = [half * (c[h] + below[h]) for h in range(2)]
    north = [half * (c[h] + above[h]) for h in range(2)]
    for i in range(16):
        for h in range(2):
            j = sub[h]
            diagonal = (east[h] + lroll(east[h], 1)) + (south[h] + north[h]) + SCREENING
            value = jnp.where(j == i, diagonal, 0.0)
            value = jnp.where(j == i + 1, -south[h], value)
            value = jnp.where(j == i - 1, -north[h], value)
            bmat[pl.ds(i * 16 + h * 8, 8), :] = value
            emat[pl.ds(i * 16 + h * 8, 8), :] = jnp.where(j == i, -east[h], 0.0)


def mat(ref, i, h, base=0):
    return ref[pl.ds(base + i * 16 + h * 8, 8), :]


def matT(ref, i, h, base=0):
    return ref[pl.ds(base + h * 128 + i, 8, stride=16), :]


def inverted(a, pivots):
    sub = [lax.broadcasted_iota(jnp.int32, (8, 128), 0) + 8 * h for h in range(2)]
    for k in range(16):
        hk = k // 8
        base = k * 16
        for h in range(2):
            pivots[pl.ds(base + h * 8, 8), :] = a[k][h]
        p = 1.0 / row_of(pivots, base + k)
        scaled = [a[k][h] * p for h in range(2)]
        rk = list(scaled)
        rk[hk] = jnp.where(sub[hk] == k, 1.0 + p, rk[hk])
        new = []
        for i in range(16):
            if i == k:
                fin = list(scaled)
                fin[hk] = jnp.where(sub[hk] == k, p, fin[hk])
                new.append(fin)
                continue
            f = row_of(pivots, base + i)
            if i < k:
                f = -f
            new.append([a[i][h] - f * rk[h] for h in range(2)])
        a = new
    return a


def put(ref, a, base=0):
    for i in range(16):
        for h in range(2):
            ref[pl.ds(base + i * 16 + h * 8, 8), :] = a[i][h]


def product(left, rights):
    outs = [[] for _ in rights]
    for i in range(16):
        acc = [[None, None] for _ in rights]
        for k in range(16):
            f = row_of(left, i * 16 + k)
            for q, right in enumerate(rights):
                for h in range(2):
                    term = f * right[k][h]
                    acc[q][h] = term if k == 0 else acc[q][h] + term
        for q in range(len(rights)):
            outs[q].append(acc[q])
    return outs


def factor(bmat, emat, gs, xs, xts, left, pivots):
    lane = lax.broadcasted_iota(jnp.int32, (8, 128), 1)
    both = [(i, h) for i in range(16) for h in range(2)]

    def body(m, _):
        d = jnp.left_shift(1, m)
        odd = jnp.bitwise_and(lane, d) != 0
        base = pl.multiple_of(m * 256, 256)
        g = inverted([[mat(bmat, i, h) for h in range(2)] for i in range(16)], pivots)
        put(gs, g, base)

        def ahead(x):
            return pltpu.roll(x, 128 - d, 1)

        for i, h in both:
            left[pl.ds(i * 16 + h * 8, 8), :] = jnp.where(odd, g[i][h], ahead(g[i][h]))
        f = [
            [jnp.where(odd, mat(emat, i, h), matT(emat, i, h)) for h in range(2)] for i in range(16)
        ]
        (x,) = product(left, [f])
        put(xs, x, base)
        for i, h in both:
            xts[pl.ds(base + i * 16 + h * 8, 8), :] = xs[pl.ds(base + h * 128 + i, 8, stride=16), :]
        for i, h in both:
            left[pl.ds(i * 16 + h * 8, 8), :] = jnp.where(odd, matT(emat, i, h), mat(emat, i, h))
        y, n = product(left, [x, [[ahead(x[i][h]) for h in range(2)] for i in range(16)]])
        even = jnp.bitwise_and(lane, 2 * d - 1) == 0
        for i, h in both:
            old = mat(bmat, i, h)
            fresh = old - (y[i][h] + pltpu.roll(y[i][h], d, 1))
            bmat[pl.ds(i * 16 + h * 8, 8), :] = jnp.where(even, fresh, old)
            emat[pl.ds(i * 16 + h * 8, 8), :] = -n[i][h]
        return 0

    lax.fori_loop(0, 5, body, 0)
    last = [
        [mat(bmat, i, h) + (mat(emat, i, h) + matT(emat, i, h)) for h in range(2)] for i in range(16)
    ]
    even = jnp.bitwise_and(lane, 31) == 0
    last = [
        [jnp.where(even, last[i][h], mat(bmat, i, h)) for h in range(2)] for i in range(16)
    ]
    put(gs, inverted(last, pivots), 5 * 256)


def times(ref, base, vec, x):
    vec[pl.ds(0, 8), :], vec[pl.ds(8, 8), :] = x[0], x[1]
    out = []
    for h in range(2):
        terms = [mat(ref, k, h, base) * row_of(vec, k) for k in range(16)]
        while len(terms) > 1:
            terms = [terms[q] + terms[q + 1] for q in range(0, len(terms), 2)]
        out.append(terms[0])
    return out


def ring_solve(r, gs, xs, xts, vecs):
    lane = lax.broadcasted_iota(jnp.int32, (8, 128), 1)
    two = range(2)
    for m in range(5):
        d = 1 << m
        odd, even = (lane & d) != 0, (lane & (2 * d - 1)) == 0
        sel = [jnp.where(odd, r[h], lroll(r[h], -d)) for h in two]
        z = times(xs, m * 256, vecs.at[m], sel)
        r = [jnp.where(even, r[h] - (z[h] + lroll(z[h], d)), r[h]) for h in two]
    x = times(gs, 5 * 256, vecs.at[5], r)
    for m in reversed(range(5)):
        d = 1 << m
        odd, now = (lane & d) != 0, (lane & (2 * d - 1)) == d
        sel = [jnp.where(odd, lroll(x[h], -d), x[h]) for h in two]
        g = times(gs, m * 256, vecs.at[6 + m], r)
        q = times(xts, m * 256, vecs.at[11 + m], sel)
        x = [jnp.where(now, g[h] - (q[h] + lroll(q[h], d)), x[h]) for h in two]
    return x


def potential_of(gath, w, sq, sq2, bmat, emat, gs, xs, xts, left, pivots, vecs):
    scale = 1.0 / 512.0
    at = [pl.ds((v // 8) * 16 + v % 8, 8, stride=64) for v in range(NV)]
    cond = [gath[s, :] * scale for s in at]
    level_weights(cond, 0, *w[0])
    c = coarsened(cond, 1)
    level_weights(c, 1, *w[1])
    c = coarsened(c, 2)
    level_weights(c, 2, *w[2])
    c = coarsened(c, 4)
    ring_matrix(to_ring(c, sq, sq2), bmat, emat)
    factor(bmat, emat, gs, xs, xts, left, pivots)
    at = [pl.ds((v // 8) * 16 + 8 + v % 8, 8, stride=64) for v in range(NV)]
    source = [gath[s, :] * scale for s in at]

    def coarse(r):
        x = ring_solve(to_ring(r, sq, sq2), gs, xs, xts, vecs)
        return from_ring(x, sq, sq2, vecs.at[16])

    x = None
    for _ in range(CYCLES):
        x = vcycle(0, source, x, w, coarse)
    return x


def stencil(pot, west, east):
    lane = lax.broadcasted_iota(jnp.int32, (8, 128), 1)
    low, high = lane == 0, lane == 127

    def slope(q):
        return jnp.where(high, 0.0, lroll(q, -1)) - jnp.where(low, 0.0, lroll(q, 1))

    uw = CAP * jnp.tanh(-0.25 * slope(west + pot))
    ue = CAP * jnp.tanh(-0.25 * slope(pot + east))
    r = east - west
    us = jnp.where(low, 0.0, CAP * jnp.tanh(0.25 * (lroll(r, 1) + r)))
    un = jnp.where(high, 0.0, lroll(us, -1))
    pos = [jnp.maximum(u, 0.0) for u in (uw, ue, us, un)]
    neg = [jnp.minimum(u, 0.0) for u in (uw, ue, us, un)]
    centre = 1.0 - (pos[1] - neg[0]) - (pos[3] - neg[2])
    return centre, pos[0], -neg[1], pos[2], -neg[3]


def solve_kernel(
    gath, ent, ent_l, ent_r, cour, dens_hbm, halo_hbm, out, pot,
    wl0, ws0, wn0, kk0, dd0, wl1, ws1, wn1, kk1, wl2, ws2, wn2, kk2,
    sq, sq2, bmat, emat, gs, xs, xts, left, pivots, vecs, whole, atab, btab, dens, halo, sem,
):
    ns, pts = out.shape[:2]
    l = lax.axis_index("lon")
    loads = [
        pltpu.make_async_copy(dens_hbm, dens, sem.at[0]),
        pltpu.make_async_copy(halo_hbm, halo, sem.at[1]),
    ]
    for c in loads:
        c.start()
    coefficient_tables(cour, atab, btab)
    w = [(wl0, ws0, wn0, kk0, dd0), (wl1, ws1, wn1, kk1, None), (wl2, ws2, wn2, kk2, None)]
    x = potential_of(gath, w, sq, sq2, bmat, emat, gs, xs, xts, left, pivots, vecs)
    for v in range(NV):
        whole[pl.ds(v, 8, stride=NV), :] = x[v]
    own = whole[pl.ds(pl.multiple_of(l * 8, 8), 8), :]
    sub = lax.broadcasted_iota(jnp.int32, (8, 128), 0)
    west = jnp.where(sub == 0, row_of(whole, lax.rem(l * 8 + 255, 256)), pltpu.roll(own, 1, 0))
    east = jnp.where(sub == 7, row_of(whole, lax.rem(l * 8 + 8, 256)), pltpu.roll(own, 7, 0))
    pot[...] = own
    cc, cw, ce, cs, cn = stencil(own, west, east)
    for c in loads:
        c.wait()

    start = []
    for s in range(ns):
        side = jnp.where(sub == 0, pltpu.roll(ent_l[s], 1, 0), pltpu.roll(ent_r[s], 7, 0))
        start.append((ent[s], side))

    def step(p, carry):
        new = []
        for s in range(ns):
            y, side = carry[s]
            a, b = row_of(atab, p * 8 + s), row_of(btab, p * 8 + s)
            y = a * y + b * dens[s, p]
            side = a * side + b * halo[s, p]
            yw = jnp.where(sub == 0, side, pltpu.roll(y, 1, 0))
            ye = jnp.where(sub == 7, side, pltpu.roll(y, 7, 0))
            out[s, p] = (cc * y + (cw * yw + ce * ye)) + (cs * lroll(y, 1) + cn * lroll(y, -1))
            new.append((y, side))
        return tuple(new)

    lax.fori_loop(0, pts, step, tuple(start))


def solve(gath, ent, ent_l, ent_r, courant, density, halo):
    ns, pts = density.shape[:2]
    vm = pl.BlockSpec(memory_space=pltpu.VMEM)
    hbm = pl.BlockSpec(memory_space=pl.ANY)

    def tiles(n):
        return pltpu.VMEM((n, 8, 128), F32)

    def rows(n):
        return pltpu.VMEM((n, 128), F32)

    levels = [tiles(33)] + [tiles(32)] * 4 + [tiles(17)] + [tiles(16)] * 3 + [tiles(9)] + [tiles(8)] * 3
    return pl.pallas_call(
        solve_kernel,
        out_shape=(
            jax.ShapeDtypeStruct(density.shape, F32),
            jax.ShapeDtypeStruct((8, 128), F32),
        ),
        in_specs=[vm] * 5 + [hbm] * 2,
        out_specs=(vm, vm),
        scratch_shapes=levels
        + [rows(128), rows(128), rows(256), rows(256), rows(6 * 256), rows(5 * 256), rows(5 * 256)]
        + [rows(256), rows(256), pltpu.VMEM((17, 16, 128), F32), rows(256)]
        + [rows(pts * 8), rows(pts * 8)]
        + [pltpu.VMEM(density.shape, F32), pltpu.VMEM(density.shape, F32)]
        + [pltpu.SemaphoreType.DMA((2,))],
        compiler_params=pltpu.CompilerParams(vmem_limit_bytes=40 * 2**20),
        name="solve",
    )(gath, ent, ent_l, ent_r, courant, density, halo)


def solution(mesh):
    def on_device(density, pedersen, wind, courant):
        gath, halo, ent, ent_l, ent_r = exchange(mesh, density, pedersen, wind, courant)
        return solve(gath.reshape(-1, 128), ent, ent_l, ent_r, courant, density, halo)

    return jax.shard_map(
        on_device,
        mesh=mesh,
        in_specs=(
            P(None, "tube", "lon", None),
            P("tube", "lon", None),
            P("tube", "lon", None),
            P(None, "tube"),
        ),
        out_specs=(P(None, "tube", "lon", None), P("lon", None)),
        check_vma=False,
    )
```

```python
import functools

import jax
import jax.numpy as jnp
from jax import lax
from jax.experimental import pallas as pl
from jax.experimental.pallas import tpu as pltpu
from jax.sharding import PartitionSpec as P

F32 = jnp.float32
SCREENING = 0.005
CAP = 0.2
NV = 32
CYCLES = 3
SCALE = 1.0 / 512.0
MESH = pl.DeviceIdType.MESH


def row_of(ref, r):
    return jnp.broadcast_to(ref[pl.ds(r, 1), :], (8, 128))


def coefficient_tables(cour, atab, btab):
    c = cour[...]
    inv = 1.0 / (1.0 + c)
    keep = c * inv
    ns, pts = c.shape
    for p in range(pts):
        atab[pl.ds(p * 8, ns), :] = jnp.broadcast_to(keep[:, p : p + 1], (ns, 128))
        btab[pl.ds(p * 8, ns), :] = jnp.broadcast_to(inv[:, p : p + 1], (ns, 128))


def lroll(x, shift):
    return pltpu.roll(x, shift % 128, x.ndim - 1)


def before(x):
    return [pltpu.roll(x[-1], 1, 0)] + x[:-1]


def after(x):
    return x[1:] + [pltpu.roll(x[0], 7, 0)]


def level_weights(cond, level, wl, ws, wn, kk, dd):
    half, step, n = 0.5 * 0.25**level, 2**level, len(cond)
    lane = lax.broadcasted_iota(jnp.int32, (8, 128), 1)
    lo, hi = lane >= step, lane < 128 - step
    west = [half * (a + b) for a, b in zip(before(cond), cond)]
    west.append(pltpu.roll(west[0], 7, 0))
    for v in range(n + 1):
        wl[v] = west[v]
    for v in range(n):
        c = cond[v]
        south = half * (c + jnp.where(lo, lroll(c, step), 0.0))
        north = half * (c + jnp.where(hi, lroll(c, -step), 0.0))
        ws[v] = jnp.where(lo, south, 0.0)
        wn[v] = jnp.where(hi, north, 0.0)
        diagonal = (west[v] + west[v + 1]) + (south + north) + SCREENING
        kk[v] = 0.8 / diagonal
        if dd is not None:
            dd[v] = diagonal


def coarsened(x, step):
    lane = lax.broadcasted_iota(jnp.int32, (8, 128), 1)
    low = (lane // step) % 2 == 0
    out = []
    for v in range(0, len(x), 2):
        y = x[v] + x[v + 1]
        out.append(0.25 * (y + jnp.where(low, lroll(y, -step), lroll(y, step))))
    return out


def pulled(x, w, level):
    wl, ws, wn = w[:3]
    step, b, a = 2**level, before(x), after(x)
    return [
        (wl[v] * b[v] + wl[v + 1] * a[v])
        + (ws[v] * lroll(x[v], step) + wn[v] * lroll(x[v], -step))
        for v in range(len(x))
    ]


def vcycle(level, rhs, start, w, coarse):
    if level == len(w):
        return coarse(rhs)
    n = len(rhs)
    kk = w[level][3]
    if start is None:
        x = [kk[v] * rhs[v] for v in range(n)]
        e = [0.2 * r + p for r, p in zip(rhs, pulled(x, w[level], level))]
    else:
        dd = w[level][4]
        p = pulled(start, w[level], level)
        x = [0.2 * start[v] + kk[v] * (rhs[v] + p[v]) for v in range(n)]
        p = pulled(x, w[level], level)
        e = [(rhs[v] - dd[v] * x[v]) + p[v] for v in range(n)]
    fix = vcycle(level + 1, coarsened(e, 2**level), None, w, coarse)
    x = [x[v] + fix[v // 2] for v in range(n)]
    p = pulled(x, w[level], level)
    return [0.2 * x[v] + kk[v] * (rhs[v] + p[v]) for v in range(n)]


def to_ring(x, sq, sq2):
    for v in range(4):
        for rep in range(4):
            sq[pl.ds(rep * 32 + v, 8, stride=4), :] = x[v]
    sq2[...] = sq[...].T
    return [sq2[pl.ds(0, 8, stride=8), :], sq2[pl.ds(64, 8, stride=8), :]]


def from_ring(x, sq, sq2, vec):
    vec[pl.ds(0, 8), :], vec[pl.ds(8, 8), :] = x[0], x[1]
    for j in range(16):
        sq[pl.ds(j * 8, 8), :] = row_of(vec, j)
    sq2[...] = sq[...].T
    return [sq2[pl.ds(v, 8, stride=4), :] for v in range(4)]


def ring_matrix(c, bmat, emat):
    sub = [lax.broadcasted_iota(jnp.int32, (8, 128), 0) + 8 * h for h in range(2)]
    half = 0.5 * 0.25**3
    east = [half * (c[h] + lroll(c[h], -1)) for h in range(2)]
    up = [pltpu.roll(c[h], 1, 0) for h in range(2)]
    dn = [pltpu.roll(c[h], 7, 0) for h in range(2)]
    first, last = sub[0] % 8 == 0, sub[0] % 8 == 7
    below = [jnp.where(first, 0.0, up[0]), jnp.where(first, up[0], up[1])]
    above = [jnp.where(last, dn[1], dn[0]), jnp.where(last, 0.0, dn[1])]
    south = [half * (c[h] + below[h]) for h in range(2)]
    north = [half * (c[h] + above[h]) for h in range(2)]
    for i in range(16):
        for h in range(2):
            j = sub[h]
            diagonal = (east[h] + lroll(east[h], 1)) + (south[h] + north[h]) + SCREENING
            value = jnp.where(j == i, diagonal, 0.0)
            value = jnp.where(j == i + 1, -south[h], value)
            value = jnp.where(j == i - 1, -north[h], value)
            bmat[pl.ds(i * 16 + h * 8, 8), :] = value
            emat[pl.ds(i * 16 + h * 8, 8), :] = jnp.where(j == i, -east[h], 0.0)


def mat(ref, i, h, base=0):
    return ref[pl.ds(base + i * 16 + h * 8, 8), :]


def matT(ref, i, h, base=0):
    return ref[pl.ds(base + h * 128 + i, 8, stride=16), :]


def inverted(a, pivots):
    sub = [lax.broadcasted_iota(jnp.int32, (8, 128), 0) + 8 * h for h in range(2)]
    for k in range(16):
        hk = k // 8
        base = k * 16
        for h in range(2):
            pivots[pl.ds(base + h * 8, 8), :] = a[k][h]
        p = 1.0 / row_of(pivots, base + k)
        scaled = [a[k][h] * p for h in range(2)]
        rk = list(scaled)
        rk[hk] = jnp.where(sub[hk] == k, 1.0 + p, rk[hk])
        new = []
        for i in range(16):
            if i == k:
                fin = list(scaled)
                fin[hk] = jnp.where(sub[hk] == k, p, fin[hk])
                new.append(fin)
                continue
            f = row_of(pivots, base + i)
            if i < k:
                f = -f
            new.append([a[i][h] - f * rk[h] for h in range(2)])
        a = new
    return a


def put(ref, a, base=0):
    for i in range(16):
        for h in range(2):
            ref[pl.ds(base + i * 16 + h * 8, 8), :] = a[i][h]


def product(left, rights):
    outs = [[] for _ in rights]
    for i in range(16):
        acc = [[None, None] for _ in rights]
        for k in range(16):
            f = row_of(left, i * 16 + k)
            for q, right in enumerate(rights):
                for h in range(2):
                    term = f * right[k][h]
                    acc[q][h] = term if k == 0 else acc[q][h] + term
        for q in range(len(rights)):
            outs[q].append(acc[q])
    return outs


def factor(bmat, emat, gs, xs, xts, left, pivots):
    lane = lax.broadcasted_iota(jnp.int32, (8, 128), 1)
    both = [(i, h) for i in range(16) for h in range(2)]

    def body(m, _):
        d = jnp.left_shift(1, m)
        odd = jnp.bitwise_and(lane, d) != 0
        base = pl.multiple_of(m * 256, 256)
        g = inverted([[mat(bmat, i, h) for h in range(2)] for i in range(16)], pivots)
        put(gs, g, base)

        def ahead(x):
            return pltpu.roll(x, 128 - d, 1)

        for i, h in both:
            left[pl.ds(i * 16 + h * 8, 8), :] = jnp.where(odd, g[i][h], ahead(g[i][h]))
        f = [
            [jnp.where(odd, mat(emat, i, h), matT(emat, i, h)) for h in range(2)] for i in range(16)
        ]
        (x,) = product(left, [f])
        put(xs, x, base)
        for i, h in both:
            xts[pl.ds(base + i * 16 + h * 8, 8), :] = xs[pl.ds(base + h * 128 + i, 8, stride=16), :]
        for i, h in both:
            left[pl.ds(i * 16 + h * 8, 8), :] = jnp.where(odd, matT(emat, i, h), mat(emat, i, h))
        y, n = product(left, [x, [[ahead(x[i][h]) for h in range(2)] for i in range(16)]])
        even = jnp.bitwise_and(lane, 2 * d - 1) == 0
        for i, h in both:
            old = mat(bmat, i, h)
            fresh = old - (y[i][h] + pltpu.roll(y[i][h], d, 1))
            bmat[pl.ds(i * 16 + h * 8, 8), :] = jnp.where(even, fresh, old)
            emat[pl.ds(i * 16 + h * 8, 8), :] = -n[i][h]
        return 0

    lax.fori_loop(0, 5, body, 0)
    last = [
        [mat(bmat, i, h) + (mat(emat, i, h) + matT(emat, i, h)) for h in range(2)] for i in range(16)
    ]
    even = jnp.bitwise_and(lane, 31) == 0
    last = [
        [jnp.where(even, last[i][h], mat(bmat, i, h)) for h in range(2)] for i in range(16)
    ]
    put(gs, inverted(last, pivots), 5 * 256)


def times(ref, base, vec, x):
    vec[pl.ds(0, 8), :], vec[pl.ds(8, 8), :] = x[0], x[1]
    out = []
    for h in range(2):
        terms = [mat(ref, k, h, base) * row_of(vec, k) for k in range(16)]
        while len(terms) > 1:
            terms = [terms[q] + terms[q + 1] for q in range(0, len(terms), 2)]
        out.append(terms[0])
    return out


def ring_solve(r, gs, xs, xts, vecs):
    lane = lax.broadcasted_iota(jnp.int32, (8, 128), 1)
    two = range(2)
    for m in range(5):
        d = 1 << m
        odd, even = (lane & d) != 0, (lane & (2 * d - 1)) == 0
        sel = [jnp.where(odd, r[h], lroll(r[h], -d)) for h in two]
        z = times(xs, m * 256, vecs.at[m], sel)
        r = [jnp.where(even, r[h] - (z[h] + lroll(z[h], d)), r[h]) for h in two]
    x = times(gs, 5 * 256, vecs.at[5], r)
    for m in reversed(range(5)):
        d = 1 << m
        odd, now = (lane & d) != 0, (lane & (2 * d - 1)) == d
        sel = [jnp.where(odd, lroll(x[h], -d), x[h]) for h in two]
        g = times(gs, m * 256, vecs.at[6 + m], r)
        q = times(xts, m * 256, vecs.at[11 + m], sel)
        x = [jnp.where(now, g[h] - (q[h] + lroll(q[h], d)), x[h]) for h in two]
    return x


def conductance_setup(gath, w, ring, mats):
    cond = [gath[pl.ds((v // 8) * 16 + v % 8, 8, stride=64), :] * SCALE for v in range(NV)]
    level_weights(cond, 0, *w[0])
    c = coarsened(cond, 1)
    level_weights(c, 1, *w[1])
    c = coarsened(c, 2)
    level_weights(c, 2, *w[2])
    c = coarsened(c, 4)
    sq, sq2, vecs = ring
    bmat, emat, gs, xs, xts, left, pivots = mats
    ring_matrix(to_ring(c, sq, sq2), bmat, emat)
    factor(bmat, emat, gs, xs, xts, left, pivots)


def cycles(gath, w, ring, mats, pot):
    sq, sq2, vecs = ring
    _, _, gs, xs, xts, _, _ = mats

    def coarse(r):
        x = ring_solve(to_ring(r, sq, sq2), gs, xs, xts, vecs)
        return from_ring(x, sq, sq2, vecs.at[16])

    def body(_, carry):
        at = [pl.ds((v // 8) * 16 + 8 + v % 8, 8, stride=64) for v in range(NV)]
        source = [gath[s, :] * SCALE for s in at]
        x = vcycle(0, source, [pot[v] for v in range(NV)], w, coarse)
        for v in range(NV):
            pot[v] = x[v]
        return carry

    for v in range(NV):
        pot[v] = jnp.zeros((8, 128), F32)
    lax.fori_loop(0, CYCLES, body, 0)


def stencil(pot, west, east):
    lane = lax.broadcasted_iota(jnp.int32, (8, 128), 1)
    low, high = lane == 0, lane == 127

    def slope(q):
        return jnp.where(high, 0.0, lroll(q, -1)) - jnp.where(low, 0.0, lroll(q, 1))

    uw = CAP * jnp.tanh(-0.25 * slope(west + pot))
    ue = CAP * jnp.tanh(-0.25 * slope(pot + east))
    r = east - west
    us = jnp.where(low, 0.0, CAP * jnp.tanh(0.25 * (lroll(r, 1) + r)))
    un = jnp.where(high, 0.0, lroll(us, -1))
    pos = [jnp.maximum(u, 0.0) for u in (uw, ue, us, un)]
    neg = [jnp.minimum(u, 0.0) for u in (uw, ue, us, un)]
    centre = 1.0 - (pos[1] - neg[0]) - (pos[3] - neg[2])
    return centre, pos[0], -neg[1], pos[2], -neg[3]


def dynamo_kernel(
    nt, nl, ped_hbm, wind_hbm, cour_hbm, dens_hbm,
    coef, pot_own, ent, ent_l, ent_r, dens, halo, atab, btab,
    ped, wind, cour, part, parts, gath, bsend, brecv, psend,
    wl0, ws0, wn0, kk0, dd0, wl1, ws1, wn1, kk1, wl2, ws2, wn2, kk2,
    sq, sq2, bmat, emat, gs, xs, xts, left, pivots, vecs, pot, whole,
    s_ld, s_t, r_t, s_l, r_l, s_h, r_h, s_b, r_b, s_p, r_p, s_e, r_e,
):
    ns, pts = dens.shape[:2]
    t, l = lax.axis_index("tube"), lax.axis_index("lon")
    loads = [
        pltpu.make_async_copy(src, dst, s_ld.at[k])
        for k, (src, dst) in enumerate(
            ((ped_hbm, ped), (wind_hbm, wind), (cour_hbm, cour), (dens_hbm, dens))
        )
    ]
    for c in loads:
        c.start()

    far_t = sorted(range(1, nt), key=lambda o: -min(o, nt - o))
    far_l = sorted(range(1, nl), key=lambda o: -min(o // 2 % 4, 4 - o // 2 % 4) - min(o // 8, 4 - o // 8))
    barrier = pltpu.get_barrier_semaphore()
    for o in far_t:
        pl.semaphore_signal(
            barrier, inc=1, device_id=(lax.rem(t + o, nt), l), device_id_type=MESH
        )
    for o in far_l:
        pl.semaphore_signal(
            barrier, inc=1, device_id=(t, lax.rem(l + o, nl)), device_id_type=MESH
        )

    loads[0].wait()
    loads[1].wait()
    csum = [ped[k] for k in range(4)]
    ssum = [ped[k] * wind[k] for k in range(4)]
    for p in range(4, pts):
        csum[p % 4] = csum[p % 4] + ped[p]
        ssum[p % 4] = ssum[p % 4] + ped[p] * wind[p]
    part[pl.ds(0, 8), :] = (csum[0] + csum[1]) + (csum[2] + csum[3])
    part[pl.ds(8, 8), :] = (ssum[0] + ssum[1]) + (ssum[2] + ssum[3])

    def remote(src, dst, ssem, rsem, to):
        c = pltpu.make_async_remote_copy(
            src_ref=src, dst_ref=dst, send_sem=ssem, recv_sem=rsem,
            device_id=to, device_id_type=MESH,
        )
        c.start()
        return c

    pl.semaphore_wait(barrier, nt + nl - 2)
    along = []
    for o in far_t:
        to = lax.rem(t + o, nt)
        along.append(remote(part, parts.at[o], s_t.at[o], r_t.at[o], (to, l)))

    right, left_l = lax.rem(l + 1, nl), lax.rem(l + nl - 1, nl)
    h0 = remote(
        dens_hbm.at[:, :, pl.ds(7, 1), :], halo.at[:, :, pl.ds(0, 1), :], s_h.at[0], r_h.at[0], (t, right)
    )
    h1 = remote(
        dens_hbm.at[:, :, pl.ds(0, 1), :], halo.at[:, :, pl.ds(7, 1), :], s_h.at[1], r_h.at[1], (t, left_l)
    )

    loads[2].wait()
    coefficient_tables(cour, atab, btab)
    loads[3].wait()

    def step(p, carry):
        out = []
        for s in range(ns):
            x, m = carry[s]
            a, b = row_of(atab, p * 8 + s), row_of(btab, p * 8 + s)
            out.append((a * x + b * dens[s, p], a * m))
        return tuple(out)

    zero, one = jnp.zeros((8, 128), F32), jnp.ones((8, 128), F32)
    ends = lax.fori_loop(0, pts, step, tuple((zero, one) for _ in range(ns)))
    for s in range(ns):
        bsend[s, 0] = ends[s][0]
        bsend[s, 1] = ends[s][1]

    mine = (t * ns + nt - 1) // nt
    owner_of = [(s * nt) // ns for s in range(ns)]
    is_owner = jnp.logical_and(mine < ns, (mine * nt) // ns == t)
    for s in range(ns):

        @pl.when(t != owner_of[s])
        def _():
            o = lax.rem(t - owner_of[s] + nt, nt)
            remote(bsend.at[s], brecv.at[o], s_b.at[s], r_b.at[o], (owner_of[s], l))

    parts[0] = part[...]
    total = None
    for c in reversed(along):
        c.wait_recv()
    for o in range(nt):
        total = parts[o] if total is None else total + parts[o]
    gath[pl.ds(pl.multiple_of(l * 16, 16), 16), :] = total
    mine_rows = gath.at[pl.ds(pl.multiple_of(l * 16, 16), 16), :]
    across = []
    for o in far_l:
        to = lax.rem(l + o, nl)
        across.append(remote(mine_rows, mine_rows, s_l.at[o], r_l.at[o], (t, to)))

    @pl.when(is_owner)
    def _():
        brecv[0] = bsend[mine]
        for o in range(1, nt):
            pltpu.make_async_copy(brecv.at[o], brecv.at[o], r_b.at[o]).wait()
        x = zero
        for k in range(nt):
            psend[k] = x
            o = lax.rem(k - t + nt, nt)
            x = brecv[o, 1] * x + brecv[o, 0]
        ent[mine] = psend[t]
        for o in far_t:
            to = lax.rem(t + o, nt)
            remote(psend.at[to], ent.at[mine], s_p.at[o], r_p.at[mine], (to, l))

    for c in across:
        c.wait_recv()

    w = [(wl0, ws0, wn0, kk0, dd0), (wl1, ws1, wn1, kk1, None), (wl2, ws2, wn2, kk2, None)]
    ring, mats = (sq, sq2, vecs), (bmat, emat, gs, xs, xts, left, pivots)
    conductance_setup(gath, w, ring, mats)

    for s in range(ns):

        @pl.when(t != owner_of[s])
        def _():
            pltpu.make_async_copy(ent.at[s], ent.at[s], r_p.at[s]).wait()

    e0 = remote(ent, ent_l, s_e.at[0], r_e.at[0], (t, right))
    e1 = remote(ent, ent_r, s_e.at[1], r_e.at[1], (t, left_l))

    cycles(gath, w, ring, mats, pot)
    for v in range(NV):
        whole[pl.ds(v, 8, stride=NV), :] = pot[v]
    own = whole[pl.ds(pl.multiple_of(l * 8, 8), 8), :]
    sub = lax.broadcasted_iota(jnp.int32, (8, 128), 0)
    west = jnp.where(sub == 0, row_of(whole, lax.rem(l * 8 + 255, 256)), pltpu.roll(own, 1, 0))
    east = jnp.where(sub == 7, row_of(whole, lax.rem(l * 8 + 8, 256)), pltpu.roll(own, 7, 0))
    pot_own[...] = own
    for k, c in enumerate(stencil(own, west, east)):
        coef[k] = c

    for c in along + across:
        c.wait_send()
    for s in range(ns):

        @pl.when(t != owner_of[s])
        def _():
            pltpu.make_async_copy(bsend.at[s], bsend.at[s], s_b.at[s]).wait()

    @pl.when(is_owner)
    def _():
        for o in range(1, nt):
            pltpu.make_async_copy(psend.at[0], psend.at[0], s_p.at[o]).wait()

    for c in (h0, h1, e0, e1):
        c.wait()


VM = pl.BlockSpec(memory_space=pltpu.VMEM)
HBM = pl.BlockSpec(memory_space=pltpu.HBM)


def tiles(*n):
    return pltpu.VMEM((*n, 8, 128), F32)


def rows(n):
    return pltpu.VMEM((n, 128), F32)


def dynamo(mesh, density, pedersen, wind, courant):
    nt, nl = mesh.shape["tube"], mesh.shape["lon"]
    ns, pts = density.shape[:2]
    dma = pltpu.SemaphoreType.DMA
    state = jax.ShapeDtypeStruct((ns, 8, 128), F32)
    table = jax.ShapeDtypeStruct((pts * 8, 128), F32)
    levels = [tiles(33)] + [tiles(32)] * 4 + [tiles(17)] + [tiles(16)] * 3 + [tiles(9)] + [tiles(8)] * 3
    return pl.pallas_call(
        functools.partial(dynamo_kernel, nt, nl),
        out_shape=(
            jax.ShapeDtypeStruct((5, 8, 128), F32),
            jax.ShapeDtypeStruct((8, 128), F32),
            state, state, state,
            jax.ShapeDtypeStruct(density.shape, F32),
            jax.ShapeDtypeStruct(density.shape, F32),
            table, table,
        ),
        in_specs=[HBM] * 4,
        out_specs=(VM,) * 9,
        scratch_shapes=[
            tiles(pts), tiles(pts), pltpu.VMEM((ns, pts), F32),
            rows(16), pltpu.VMEM((nt, 16, 128), F32), rows(512),
            tiles(ns, 2), tiles(nt, 2), tiles(nt),
        ]
        + levels
        + [rows(128), rows(128), rows(256), rows(256), rows(6 * 256), rows(5 * 256), rows(5 * 256)]
        + [rows(256), rows(256), pltpu.VMEM((17, 16, 128), F32), tiles(NV), rows(256)]
        + [
            dma((4,)), dma((nt,)), dma((nt,)), dma((nl,)), dma((nl,)), dma((2,)), dma((2,)),
            dma((ns,)), dma((nt,)), dma((nt,)), dma((ns,)), dma((2,)), dma((2,)),
        ],
        compiler_params=pltpu.CompilerParams(
            collective_id=0, has_side_effects=True, vmem_limit_bytes=40 * 2**20
        ),
        name="dynamo",
    )(pedersen, wind, courant, density)


def transport_kernel(coef, pot_in, ent, ent_l, ent_r, dens, halo, atab, btab, out, pot):
    ns, pts = out.shape[:2]
    pot[...] = pot_in[...]
    cc, cw, ce, cs, cn = (coef[k] for k in range(5))
    sub = lax.broadcasted_iota(jnp.int32, (8, 128), 0)
    start = []
    for s in range(ns):
        side = jnp.where(sub == 0, pltpu.roll(ent_l[s], 1, 0), pltpu.roll(ent_r[s], 7, 0))
        start.append((ent[s], side))

    def step(p, carry):
        new = []
        for s in range(ns):
            y, side = carry[s]
            a, b = row_of(atab, p * 8 + s), row_of(btab, p * 8 + s)
            y = a * y + b * dens[s, p]
            side = a * side + b * halo[s, p]
            yw = jnp.where(sub == 0, side, pltpu.roll(y, 1, 0))
            ye = jnp.where(sub == 7, side, pltpu.roll(y, 7, 0))
            out[s, p] = (cc * y + (cw * yw + ce * ye)) + (cs * lroll(y, 1) + cn * lroll(y, -1))
            new.append((y, side))
        return tuple(new)

    lax.fori_loop(0, pts, step, tuple(start))


def transport(coef, pot, ent, ent_l, ent_r, density, halo, atab, btab):
    return pl.pallas_call(
        transport_kernel,
        out_shape=(
            jax.ShapeDtypeStruct(density.shape, F32),
            jax.ShapeDtypeStruct((8, 128), F32),
        ),
        in_specs=[VM] * 9,
        out_specs=(VM, VM),
        compiler_params=pltpu.CompilerParams(vmem_limit_bytes=24 * 2**20),
        name="transport",
    )(coef, pot, ent, ent_l, ent_r, density, halo, atab, btab)


def solution(mesh):
    def on_device(density, pedersen, wind, courant):
        args = (density, pedersen, wind, courant)
        args = (pltpu.with_memory_space_constraint(x, pltpu.HBM) for x in args)
        return transport(*dynamo(mesh, *args))

    return jax.shard_map(
        on_device,
        mesh=mesh,
        in_specs=(
            P(None, "tube", "lon", None),
            P("tube", "lon", None),
            P("tube", "lon", None),
            P(None, "tube"),
        ),
        out_specs=(P(None, "tube", "lon", None), P("lon", None)),
        check_vma=False,
    )
```

```python
import functools

import jax
import jax.numpy as jnp
from jax import lax
from jax.experimental import pallas as pl
from jax.experimental.pallas import tpu as pltpu
from jax.sharding import PartitionSpec as P

F32 = jnp.float32
SCREENING = 0.005
CAP = 0.2
NV = 32
CYCLES = 3
SCALE = 1.0 / 512.0
MESH = pl.DeviceIdType.MESH


def row_of(ref, r):
    return jnp.broadcast_to(ref[pl.ds(r, 1), :], (8, 128))


def coefficient_tables(cour, atab, btab):
    c = cour[...]
    inv = 1.0 / (1.0 + c)
    keep = c * inv
    ns, pts = c.shape
    for p in range(pts):
        atab[pl.ds(p * 8, ns), :] = jnp.broadcast_to(keep[:, p : p + 1], (ns, 128))
        btab[pl.ds(p * 8, ns), :] = jnp.broadcast_to(inv[:, p : p + 1], (ns, 128))


def lroll(x, shift):
    return pltpu.roll(x, shift % 128, x.ndim - 1)


def before(x):
    return [pltpu.roll(x[-1], 1, 0)] + x[:-1]


def after(x):
    return x[1:] + [pltpu.roll(x[0], 7, 0)]


def level_weights(cond, level, wl, ws, wn, kk, dd):
    half, step, n = 0.5 * 0.25**level, 2**level, len(cond)
    lane = lax.broadcasted_iota(jnp.int32, (8, 128), 1)
    lo, hi = lane >= step, lane < 128 - step
    west = [half * (a + b) for a, b in zip(before(cond), cond)]
    west.append(pltpu.roll(west[0], 7, 0))
    for v in range(n + 1):
        wl[v] = west[v]
    for v in range(n):
        c = cond[v]
        south = half * (c + jnp.where(lo, lroll(c, step), 0.0))
        north = half * (c + jnp.where(hi, lroll(c, -step), 0.0))
        ws[v] = jnp.where(lo, south, 0.0)
        wn[v] = jnp.where(hi, north, 0.0)
        diagonal = (west[v] + west[v + 1]) + (south + north) + SCREENING
        kk[v] = 0.8 / diagonal
        if dd is not None:
            dd[v] = diagonal


def coarsened(x, step):
    lane = lax.broadcasted_iota(jnp.int32, (8, 128), 1)
    low = (lane // step) % 2 == 0
    out = []
    for v in range(0, len(x), 2):
        y = x[v] + x[v + 1]
        out.append(0.25 * (y + jnp.where(low, lroll(y, -step), lroll(y, step))))
    return out


def pulled(x, w, level):
    wl, ws, wn = w[:3]
    step, b, a = 2**level, before(x), after(x)
    return [
        (wl[v] * b[v] + wl[v + 1] * a[v])
        + (ws[v] * lroll(x[v], step) + wn[v] * lroll(x[v], -step))
        for v in range(len(x))
    ]


def vcycle(level, rhs, start, w, coarse):
    if level == len(w):
        return coarse(rhs)
    n = len(rhs)
    kk = w[level][3]
    if start is None:
        x = [kk[v] * rhs[v] for v in range(n)]
        e = [0.2 * r + p for r, p in zip(rhs, pulled(x, w[level], level))]
    else:
        dd = w[level][4]
        p = pulled(start, w[level], level)
        x = [0.2 * start[v] + kk[v] * (rhs[v] + p[v]) for v in range(n)]
        p = pulled(x, w[level], level)
        e = [(rhs[v] - dd[v] * x[v]) + p[v] for v in range(n)]
    fix = vcycle(level + 1, coarsened(e, 2**level), None, w, coarse)
    x = [x[v] + fix[v // 2] for v in range(n)]
    p = pulled(x, w[level], level)
    return [0.2 * x[v] + kk[v] * (rhs[v] + p[v]) for v in range(n)]


def to_ring(x, sq, sq2):
    for v in range(4):
        for rep in range(4):
            sq[pl.ds(rep * 32 + v, 8, stride=4), :] = x[v]
    sq2[...] = sq[...].T
    return [sq2[pl.ds(0, 8, stride=8), :], sq2[pl.ds(64, 8, stride=8), :]]


def from_ring(x, sq, sq2, vec):
    vec[pl.ds(0, 8), :], vec[pl.ds(8, 8), :] = x[0], x[1]
    for j in range(16):
        sq[pl.ds(j * 8, 8), :] = row_of(vec, j)
    sq2[...] = sq[...].T
    return [sq2[pl.ds(v, 8, stride=4), :] for v in range(4)]


def ring_matrix(c, bmat, emat):
    sub = [lax.broadcasted_iota(jnp.int32, (8, 128), 0) + 8 * h for h in range(2)]
    half = 0.5 * 0.25**3
    east = [half * (c[h] + lroll(c[h], -1)) for h in range(2)]
    up = [pltpu.roll(c[h], 1, 0) for h in range(2)]
    dn = [pltpu.roll(c[h], 7, 0) for h in range(2)]
    first, last = sub[0] % 8 == 0, sub[0] % 8 == 7
    below = [jnp.where(first, 0.0, up[0]), jnp.where(first, up[0], up[1])]
    above = [jnp.where(last, dn[1], dn[0]), jnp.where(last, 0.0, dn[1])]
    south = [half * (c[h] + below[h]) for h in range(2)]
    north = [half * (c[h] + above[h]) for h in range(2)]
    for i in range(16):
        for h in range(2):
            j = sub[h]
            diagonal = (east[h] + lroll(east[h], 1)) + (south[h] + north[h]) + SCREENING
            value = jnp.where(j == i, diagonal, 0.0)
            value = jnp.where(j == i + 1, -south[h], value)
            value = jnp.where(j == i - 1, -north[h], value)
            bmat[pl.ds(i * 16 + h * 8, 8), :] = value
            emat[pl.ds(i * 16 + h * 8, 8), :] = jnp.where(j == i, -east[h], 0.0)


def mat(ref, i, h, base=0):
    return ref[pl.ds(base + i * 16 + h * 8, 8), :]


def matT(ref, i, h, base=0):
    return ref[pl.ds(base + h * 128 + i, 8, stride=16), :]


def inverted(a, pivots):
    sub = [lax.broadcasted_iota(jnp.int32, (8, 128), 0) + 8 * h for h in range(2)]
    for k in range(16):
        hk = k // 8
        base = k * 16
        for h in range(2):
            pivots[pl.ds(base + h * 8, 8), :] = a[k][h]
        p = 1.0 / row_of(pivots, base + k)
        scaled = [a[k][h] * p for h in range(2)]
        rk = list(scaled)
        rk[hk] = jnp.where(sub[hk] == k, 1.0 + p, rk[hk])
        new = []
        for i in range(16):
            if i == k:
                fin = list(scaled)
                fin[hk] = jnp.where(sub[hk] == k, p, fin[hk])
                new.append(fin)
                continue
            f = row_of(pivots, base + i)
            if i < k:
                f = -f
            new.append([a[i][h] - f * rk[h] for h in range(2)])
        a = new
    return a


def put(ref, a, base=0):
    for i in range(16):
        for h in range(2):
            ref[pl.ds(base + i * 16 + h * 8, 8), :] = a[i][h]


def packed_product(left, right, count):
    out = []
    for i in range(16):
        acc = [row_of(left, i * 16 + k) * right[k] for k in range(count)]
        while len(acc) > 1:
            acc = [acc[q] + acc[q + 1] for q in range(0, len(acc), 2)]
        out.append(acc[0])
    return out


def factor(bmat, emat, ps, qs, gf, left, left2, pivots):
    lane = lax.broadcasted_iota(jnp.int32, (8, 128), 1)
    group = lane // 32
    both = [(i, h) for i in range(16) for h in range(2)]
    two = range(2)

    def by_group(a, b, c, d):
        return jnp.where(group < 2, jnp.where(group == 0, a, b), jnp.where(group == 2, c, d))

    def spread(y):
        r = [y] + [lroll(y, 32 * q) for q in range(1, 4)]
        return [by_group(*(r[(g - c) % 4] for g in range(4))) for c in range(4)]

    def body(m, _):
        d = jnp.left_shift(1, m)
        base = pl.multiple_of(m * 256, 256)

        def ahead(x):
            return pltpu.roll(x, 128 - d, 1)

        def behind(x):
            return pltpu.roll(x, d, 1)

        g = inverted([[mat(bmat, i, h) for h in two] for i in range(16)], pivots)
        u = [[mat(emat, i, h) for h in two] for i in range(16)]
        ut = [[matT(emat, i, h) for h in two] for i in range(16)]
        for i, h in both:
            left[pl.ds(i * 16 + h * 8, 8), :] = jnp.where(group < 2, g[i][h], ahead(g[i][h]))
        for i in range(16):
            left2[pl.ds(i * 16, 8), :] = jnp.where(group < 2, ut[i][0], ut[i][1])
        quarters = [
            spread(y)
            for y in packed_product(left, [by_group(*u[k], *ut[k]) for k in range(16)], 16)
        ]
        q = [y[:2] for y in quarters]
        p = [y[2:] for y in quarters]
        put(ps, p, base)
        put(qs, [[behind(q[i][h]) for h in two] for i in range(16)], base)
        right = [by_group(*p[k], *(ahead(q[k][h]) for h in two)) for k in range(16)]
        first = [spread(y) for y in packed_product(emat, right, 16)]
        right = [by_group(*q[k], *q[k + 8]) for k in range(8)]
        second = []
        for y in packed_product(left2, right, 8):
            y = y + lroll(y, 64)
            z = lroll(y, 32)
            flip = group % 2 == 0
            second.append([jnp.where(flip, y, z), jnp.where(flip, z, y)])
        for i, h in both:
            rows_at = pl.ds(i * 16 + h * 8, 8)
            bmat[rows_at, :] = bmat[rows_at, :] - (first[i][h] + behind(second[i][h]))
            emat[rows_at, :] = -first[i][2 + h]
        return 0

    lax.fori_loop(0, 5, body, 0)
    last = [[mat(bmat, i, h) + (mat(emat, i, h) + matT(emat, i, h)) for h in two] for i in range(16)]
    put(gf, inverted(last, pivots))


def times(ref, base, vec, x):
    vec[pl.ds(0, 8), :], vec[pl.ds(8, 8), :] = x[0], x[1]
    out = []
    for h in range(2):
        terms = [mat(ref, k, h, base) * row_of(vec, k) for k in range(16)]
        while len(terms) > 1:
            terms = [terms[q] + terms[q + 1] for q in range(0, len(terms), 2)]
        out.append(terms[0])
    return out


def ring_solve(r, ps, qs, gf, vecs):
    for m in range(5):
        d = 1 << m
        p = times(ps, m * 256, vecs.at[2 * m], [lroll(r[h], -d) for h in range(2)])
        q = times(qs, m * 256, vecs.at[2 * m + 1], [lroll(r[h], d) for h in range(2)])
        r = [r[h] - (p[h] + q[h]) for h in range(2)]
    return times(gf, 0, vecs.at[10], r)


def conductance_setup(gath, w, ring, mats):
    cond = [gath[pl.ds((v // 8) * 16 + v % 8, 8, stride=64), :] * SCALE for v in range(NV)]
    level_weights(cond, 0, *w[0])
    c = coarsened(cond, 1)
    level_weights(c, 1, *w[1])
    c = coarsened(c, 2)
    level_weights(c, 2, *w[2])
    c = coarsened(c, 4)
    sq, sq2, vecs = ring
    bmat, emat, ps, qs, gf, left, left2, pivots = mats
    ring_matrix(to_ring(c, sq, sq2), bmat, emat)
    factor(bmat, emat, ps, qs, gf, left, left2, pivots)


def cycles(gath, w, ring, mats, pot):
    sq, sq2, vecs = ring
    ps, qs, gf = mats[2:5]

    def coarse(r):
        x = ring_solve(to_ring(r, sq, sq2), ps, qs, gf, vecs)
        return from_ring(x, sq, sq2, vecs.at[11])

    def body(_, carry):
        at = [pl.ds((v // 8) * 16 + 8 + v % 8, 8, stride=64) for v in range(NV)]
        source = [gath[s, :] * SCALE for s in at]
        x = vcycle(0, source, [pot[v] for v in range(NV)], w, coarse)
        for v in range(NV):
            pot[v] = x[v]
        return carry

    for v in range(NV):
        pot[v] = jnp.zeros((8, 128), F32)
    lax.fori_loop(0, CYCLES, body, 0)


def stencil(pot, west, east):
    lane = lax.broadcasted_iota(jnp.int32, (8, 128), 1)
    low, high = lane == 0, lane == 127

    def slope(q):
        return jnp.where(high, 0.0, lroll(q, -1)) - jnp.where(low, 0.0, lroll(q, 1))

    uw = CAP * jnp.tanh(-0.25 * slope(west + pot))
    ue = CAP * jnp.tanh(-0.25 * slope(pot + east))
    r = east - west
    us = jnp.where(low, 0.0, CAP * jnp.tanh(0.25 * (lroll(r, 1) + r)))
    un = jnp.where(high, 0.0, lroll(us, -1))
    pos = [jnp.maximum(u, 0.0) for u in (uw, ue, us, un)]
    neg = [jnp.minimum(u, 0.0) for u in (uw, ue, us, un)]
    centre = 1.0 - (pos[1] - neg[0]) - (pos[3] - neg[2])
    return centre, pos[0], -neg[1], pos[2], -neg[3]


def dynamo_kernel(
    nt, nl, ped_hbm, wind_hbm, cour_hbm, dens_hbm,
    coef, pot_own, ent, ent_l, ent_r, dens, halo, atab, btab,
    ped, wind, cour, part, parts, gath, bsend, brecv, psend,
    wl0, ws0, wn0, kk0, dd0, wl1, ws1, wn1, kk1, wl2, ws2, wn2, kk2,
    sq, sq2, bmat, emat, ps, qs, gf, left, left2, pivots, vecs, pot, whole,
    s_ld, s_t, r_t, s_l, r_l, s_h, r_h, s_b, r_b, s_p, r_p, s_e, r_e,
):
    ns, pts = dens.shape[:2]
    t, l = lax.axis_index("tube"), lax.axis_index("lon")
    loads = [
        pltpu.make_async_copy(src, dst, s_ld.at[k])
        for k, (src, dst) in enumerate(
            ((ped_hbm, ped), (wind_hbm, wind), (cour_hbm, cour), (dens_hbm, dens))
        )
    ]
    for c in loads:
        c.start()

    far_t = sorted(range(1, nt), key=lambda o: -min(o, nt - o))
    far_l = sorted(range(1, nl), key=lambda o: -min(o // 2 % 4, 4 - o // 2 % 4) - min(o // 8, 4 - o // 8))
    barrier = pltpu.get_barrier_semaphore()
    for o in far_t:
        pl.semaphore_signal(
            barrier, inc=1, device_id=(lax.rem(t + o, nt), l), device_id_type=MESH
        )
    for o in far_l:
        pl.semaphore_signal(
            barrier, inc=1, device_id=(t, lax.rem(l + o, nl)), device_id_type=MESH
        )

    loads[0].wait()
    loads[1].wait()
    csum = [ped[k] for k in range(4)]
    ssum = [ped[k] * wind[k] for k in range(4)]
    for p in range(4, pts):
        csum[p % 4] = csum[p % 4] + ped[p]
        ssum[p % 4] = ssum[p % 4] + ped[p] * wind[p]
    part[pl.ds(0, 8), :] = (csum[0] + csum[1]) + (csum[2] + csum[3])
    part[pl.ds(8, 8), :] = (ssum[0] + ssum[1]) + (ssum[2] + ssum[3])

    def remote(src, dst, ssem, rsem, to):
        c = pltpu.make_async_remote_copy(
            src_ref=src, dst_ref=dst, send_sem=ssem, recv_sem=rsem,
            device_id=to, device_id_type=MESH,
        )
        c.start()
        return c

    pl.semaphore_wait(barrier, nt + nl - 2)
    along = []
    for o in far_t:
        to = lax.rem(t + o, nt)
        along.append(remote(part, parts.at[o], s_t.at[o], r_t.at[o], (to, l)))

    right, left_l = lax.rem(l + 1, nl), lax.rem(l + nl - 1, nl)
    h0 = remote(
        dens_hbm.at[:, :, pl.ds(7, 1), :], halo.at[:, :, pl.ds(0, 1), :], s_h.at[0], r_h.at[0], (t, right)
    )
    h1 = remote(
        dens_hbm.at[:, :, pl.ds(0, 1), :], halo.at[:, :, pl.ds(7, 1), :], s_h.at[1], r_h.at[1], (t, left_l)
    )

    loads[2].wait()
    coefficient_tables(cour, atab, btab)
    loads[3].wait()

    def step(p, carry):
        out = []
        for s in range(ns):
            x, m = carry[s]
            a, b = row_of(atab, p * 8 + s), row_of(btab, p * 8 + s)
            out.append((a * x + b * dens[s, p], a * m))
        return tuple(out)

    zero, one = jnp.zeros((8, 128), F32), jnp.ones((8, 128), F32)
    ends = lax.fori_loop(0, pts, step, tuple((zero, one) for _ in range(ns)))
    for s in range(ns):
        bsend[s, 0] = ends[s][0]
        bsend[s, 1] = ends[s][1]

    mine = (t * ns + nt - 1) // nt
    owner_of = [(s * nt) // ns for s in range(ns)]
    is_owner = jnp.logical_and(mine < ns, (mine * nt) // ns == t)
    for s in range(ns):

        @pl.when(t != owner_of[s])
        def _():
            o = lax.rem(t - owner_of[s] + nt, nt)
            remote(bsend.at[s], brecv.at[o], s_b.at[s], r_b.at[o], (owner_of[s], l))

    parts[0] = part[...]
    total = None
    for c in reversed(along):
        c.wait_recv()
    for o in range(nt):
        total = parts[o] if total is None else total + parts[o]
    gath[pl.ds(pl.multiple_of(l * 16, 16), 16), :] = total
    mine_rows = gath.at[pl.ds(pl.multiple_of(l * 16, 16), 16), :]
    across = []
    for o in far_l:
        to = lax.rem(l + o, nl)
        across.append(remote(mine_rows, mine_rows, s_l.at[o], r_l.at[o], (t, to)))

    @pl.when(is_owner)
    def _():
        brecv[0] = bsend[mine]
        for o in range(1, nt):
            pltpu.make_async_copy(brecv.at[o], brecv.at[o], r_b.at[o]).wait()
        x = zero
        for k in range(nt):
            psend[k] = x
            o = lax.rem(k - t + nt, nt)
            x = brecv[o, 1] * x + brecv[o, 0]
        ent[mine] = psend[t]
        for o in far_t:
            to = lax.rem(t + o, nt)
            remote(psend.at[to], ent.at[mine], s_p.at[o], r_p.at[mine], (to, l))

    for c in across:
        c.wait_recv()

    w = [(wl0, ws0, wn0, kk0, dd0), (wl1, ws1, wn1, kk1, None), (wl2, ws2, wn2, kk2, None)]
    ring, mats = (sq, sq2, vecs), (bmat, emat, ps, qs, gf, left, left2, pivots)
    conductance_setup(gath, w, ring, mats)

    for s in range(ns):

        @pl.when(t != owner_of[s])
        def _():
            pltpu.make_async_copy(ent.at[s], ent.at[s], r_p.at[s]).wait()

    e0 = remote(ent, ent_l, s_e.at[0], r_e.at[0], (t, right))
    e1 = remote(ent, ent_r, s_e.at[1], r_e.at[1], (t, left_l))

    cycles(gath, w, ring, mats, pot)
    for v in range(NV):
        whole[pl.ds(v, 8, stride=NV), :] = pot[v]
    own = whole[pl.ds(pl.multiple_of(l * 8, 8), 8), :]
    sub = lax.broadcasted_iota(jnp.int32, (8, 128), 0)
    west = jnp.where(sub == 0, row_of(whole, lax.rem(l * 8 + 255, 256)), pltpu.roll(own, 1, 0))
    east = jnp.where(sub == 7, row_of(whole, lax.rem(l * 8 + 8, 256)), pltpu.roll(own, 7, 0))
    pot_own[...] = own
    for k, c in enumerate(stencil(own, west, east)):
        coef[k] = c

    for c in along + across:
        c.wait_send()
    for s in range(ns):

        @pl.when(t != owner_of[s])
        def _():
            pltpu.make_async_copy(bsend.at[s], bsend.at[s], s_b.at[s]).wait()

    @pl.when(is_owner)
    def _():
        for o in range(1, nt):
            pltpu.make_async_copy(psend.at[0], psend.at[0], s_p.at[o]).wait()

    for c in (h0, h1, e0, e1):
        c.wait()


VM = pl.BlockSpec(memory_space=pltpu.VMEM)
HBM = pl.BlockSpec(memory_space=pltpu.HBM)


def tiles(*n):
    return pltpu.VMEM((*n, 8, 128), F32)


def rows(n):
    return pltpu.VMEM((n, 128), F32)


def dynamo(mesh, density, pedersen, wind, courant):
    nt, nl = mesh.shape["tube"], mesh.shape["lon"]
    ns, pts = density.shape[:2]
    dma = pltpu.SemaphoreType.DMA
    state = jax.ShapeDtypeStruct((ns, 8, 128), F32)
    table = jax.ShapeDtypeStruct((pts * 8, 128), F32)
    levels = [tiles(33)] + [tiles(32)] * 4 + [tiles(17)] + [tiles(16)] * 3 + [tiles(9)] + [tiles(8)] * 3
    return pl.pallas_call(
        functools.partial(dynamo_kernel, nt, nl),
        out_shape=(
            jax.ShapeDtypeStruct((5, 8, 128), F32),
            jax.ShapeDtypeStruct((8, 128), F32),
            state, state, state,
            jax.ShapeDtypeStruct(density.shape, F32),
            jax.ShapeDtypeStruct(density.shape, F32),
            table, table,
        ),
        in_specs=[HBM] * 4,
        out_specs=(VM,) * 9,
        scratch_shapes=[
            tiles(pts), tiles(pts), pltpu.VMEM((ns, pts), F32),
            rows(16), pltpu.VMEM((nt, 16, 128), F32), rows(512),
            tiles(ns, 2), tiles(nt, 2), tiles(nt),
        ]
        + levels
        + [rows(128), rows(128), rows(256), rows(256), rows(5 * 256), rows(5 * 256), rows(256)]
        + [rows(256), rows(256), rows(256), pltpu.VMEM((12, 16, 128), F32), tiles(NV), rows(256)]
        + [
            dma((4,)), dma((nt,)), dma((nt,)), dma((nl,)), dma((nl,)), dma((2,)), dma((2,)),
            dma((ns,)), dma((nt,)), dma((nt,)), dma((ns,)), dma((2,)), dma((2,)),
        ],
        compiler_params=pltpu.CompilerParams(
            collective_id=0, has_side_effects=True, vmem_limit_bytes=40 * 2**20
        ),
        name="dynamo",
    )(pedersen, wind, courant, density)


def transport_kernel(coef, pot_in, ent, ent_l, ent_r, dens, halo, atab, btab, out, pot):
    ns, pts = out.shape[:2]
    pot[...] = pot_in[...]
    cc, cw, ce, cs, cn = (coef[k] for k in range(5))
    sub = lax.broadcasted_iota(jnp.int32, (8, 128), 0)
    start = []
    for s in range(ns):
        side = jnp.where(sub == 0, pltpu.roll(ent_l[s], 1, 0), pltpu.roll(ent_r[s], 7, 0))
        start.append((ent[s], side))

    def step(p, carry):
        new = []
        for s in range(ns):
            y, side = carry[s]
            a, b = row_of(atab, p * 8 + s), row_of(btab, p * 8 + s)
            y = a * y + b * dens[s, p]
            side = a * side + b * halo[s, p]
            yw = jnp.where(sub == 0, side, pltpu.roll(y, 1, 0))
            ye = jnp.where(sub == 7, side, pltpu.roll(y, 7, 0))
            out[s, p] = (cc * y + (cw * yw + ce * ye)) + (cs * lroll(y, 1) + cn * lroll(y, -1))
            new.append((y, side))
        return tuple(new)

    lax.fori_loop(0, pts, step, tuple(start))


def transport(coef, pot, ent, ent_l, ent_r, density, halo, atab, btab):
    return pl.pallas_call(
        transport_kernel,
        out_shape=(
            jax.ShapeDtypeStruct(density.shape, F32),
            jax.ShapeDtypeStruct((8, 128), F32),
        ),
        in_specs=[VM] * 9,
        out_specs=(VM, VM),
        compiler_params=pltpu.CompilerParams(vmem_limit_bytes=24 * 2**20),
        name="transport",
    )(coef, pot, ent, ent_l, ent_r, density, halo, atab, btab)


def solution(mesh):
    def on_device(density, pedersen, wind, courant):
        args = (density, pedersen, wind, courant)
        args = (pltpu.with_memory_space_constraint(x, pltpu.HBM) for x in args)
        return transport(*dynamo(mesh, *args))

    return jax.shard_map(
        on_device,
        mesh=mesh,
        in_specs=(
            P(None, "tube", "lon", None),
            P("tube", "lon", None),
            P("tube", "lon", None),
            P(None, "tube"),
        ),
        out_specs=(P(None, "tube", "lon", None), P("lon", None)),
        check_vma=False,
    )
```

```python
import functools

import jax
import jax.numpy as jnp
from jax import lax
from jax.experimental import pallas as pl
from jax.experimental.pallas import tpu as pltpu
from jax.sharding import PartitionSpec as P

F32 = jnp.float32
SCREENING = 0.005
CAP = 0.2
NV = 32
CYCLES = 3
CHUNK = 8
SCALE = 1.0 / 512.0
MESH = pl.DeviceIdType.MESH


def row_of(ref, r):
    return jnp.broadcast_to(ref[pl.ds(r, 1), :], (8, 128))


def coefficient_tables(cour, atab, btab):
    c = cour[...]
    inv = 1.0 / (1.0 + c)
    keep = c * inv
    ns, pts = c.shape
    for p in range(pts):
        atab[pl.ds(p * 8, ns), :] = jnp.broadcast_to(keep[:, p : p + 1], (ns, 128))
        btab[pl.ds(p * 8, ns), :] = jnp.broadcast_to(inv[:, p : p + 1], (ns, 128))


def lroll(x, shift):
    return pltpu.roll(x, shift % 128, x.ndim - 1)


def before(x):
    return [pltpu.roll(x[-1], 1, 0)] + x[:-1]


def after(x):
    return x[1:] + [pltpu.roll(x[0], 7, 0)]


def level_weights(cond, level, wl, ws, wn, kk, dd):
    half, step, n = 0.5 * 0.25**level, 2**level, len(cond)
    lane = lax.broadcasted_iota(jnp.int32, (8, 128), 1)
    lo, hi = lane >= step, lane < 128 - step
    west = [half * (a + b) for a, b in zip(before(cond), cond)]
    west.append(pltpu.roll(west[0], 7, 0))
    for v in range(n + 1):
        wl[v] = west[v]
    for v in range(n):
        c = cond[v]
        south = half * (c + jnp.where(lo, lroll(c, step), 0.0))
        north = half * (c + jnp.where(hi, lroll(c, -step), 0.0))
        ws[v] = jnp.where(lo, south, 0.0)
        wn[v] = jnp.where(hi, north, 0.0)
        diagonal = (west[v] + west[v + 1]) + (south + north) + SCREENING
        kk[v] = 0.8 / diagonal
        if dd is not None:
            dd[v] = diagonal


def coarsened(x, step):
    lane = lax.broadcasted_iota(jnp.int32, (8, 128), 1)
    low = (lane // step) % 2 == 0
    out = []
    for v in range(0, len(x), 2):
        y = x[v] + x[v + 1]
        out.append(0.25 * (y + jnp.where(low, lroll(y, -step), lroll(y, step))))
    return out


def pulled(x, w, level):
    wl, ws, wn = w[:3]
    step, b, a = 2**level, before(x), after(x)
    return [
        (wl[v] * b[v] + wl[v + 1] * a[v])
        + (ws[v] * lroll(x[v], step) + wn[v] * lroll(x[v], -step))
        for v in range(len(x))
    ]


def vcycle(level, rhs, start, w, coarse):
    if level == len(w):
        return coarse(rhs)
    n = len(rhs)
    kk = w[level][3]
    if start is None:
        x = [kk[v] * rhs[v] for v in range(n)]
        e = [0.2 * r + p for r, p in zip(rhs, pulled(x, w[level], level))]
    else:
        dd = w[level][4]
        p = pulled(start, w[level], level)
        x = [0.2 * start[v] + kk[v] * (rhs[v] + p[v]) for v in range(n)]
        p = pulled(x, w[level], level)
        e = [(rhs[v] - dd[v] * x[v]) + p[v] for v in range(n)]
    fix = vcycle(level + 1, coarsened(e, 2**level), None, w, coarse)
    x = [x[v] + fix[v // 2] for v in range(n)]
    p = pulled(x, w[level], level)
    return [0.2 * x[v] + kk[v] * (rhs[v] + p[v]) for v in range(n)]


def to_ring(x, sq, sq2):
    for v in range(4):
        for rep in range(4):
            sq[pl.ds(rep * 32 + v, 8, stride=4), :] = x[v]
    sq2[...] = sq[...].T
    return [sq2[pl.ds(0, 8, stride=8), :], sq2[pl.ds(64, 8, stride=8), :]]


def from_ring(x, sq, sq2, vec):
    vec[pl.ds(0, 8), :], vec[pl.ds(8, 8), :] = x[0], x[1]
    for j in range(16):
        sq[pl.ds(j * 8, 8), :] = row_of(vec, j)
    sq2[...] = sq[...].T
    return [sq2[pl.ds(v, 8, stride=4), :] for v in range(4)]


def ring_matrix(c, bmat, emat):
    sub = [lax.broadcasted_iota(jnp.int32, (8, 128), 0) + 8 * h for h in range(2)]
    half = 0.5 * 0.25**3
    east = [half * (c[h] + lroll(c[h], -1)) for h in range(2)]
    up = [pltpu.roll(c[h], 1, 0) for h in range(2)]
    dn = [pltpu.roll(c[h], 7, 0) for h in range(2)]
    first, last = sub[0] % 8 == 0, sub[0] % 8 == 7
    below = [jnp.where(first, 0.0, up[0]), jnp.where(first, up[0], up[1])]
    above = [jnp.where(last, dn[1], dn[0]), jnp.where(last, 0.0, dn[1])]
    south = [half * (c[h] + below[h]) for h in range(2)]
    north = [half * (c[h] + above[h]) for h in range(2)]
    for i in range(16):
        for h in range(2):
            j = sub[h]
            diagonal = (east[h] + lroll(east[h], 1)) + (south[h] + north[h]) + SCREENING
            value = jnp.where(j == i, diagonal, 0.0)
            value = jnp.where(j == i + 1, -south[h], value)
            value = jnp.where(j == i - 1, -north[h], value)
            bmat[pl.ds(i * 16 + h * 8, 8), :] = value
            emat[pl.ds(i * 16 + h * 8, 8), :] = jnp.where(j == i, -east[h], 0.0)


def mat(ref, i, h, base=0):
    return ref[pl.ds(base + i * 16 + h * 8, 8), :]


def matT(ref, i, h, base=0):
    return ref[pl.ds(base + h * 128 + i, 8, stride=16), :]


def inverted(a, pivots):
    sub = [lax.broadcasted_iota(jnp.int32, (8, 128), 0) + 8 * h for h in range(2)]
    for k in range(16):
        hk = k // 8
        base = k * 16
        for h in range(2):
            pivots[pl.ds(base + h * 8, 8), :] = a[k][h]
        p = 1.0 / row_of(pivots, base + k)
        scaled = [a[k][h] * p for h in range(2)]
        rk = list(scaled)
        rk[hk] = jnp.where(sub[hk] == k, 1.0 + p, rk[hk])
        new = []
        for i in range(16):
            if i == k:
                fin = list(scaled)
                fin[hk] = jnp.where(sub[hk] == k, p, fin[hk])
                new.append(fin)
                continue
            f = row_of(pivots, base + i)
            if i < k:
                f = -f
            new.append([a[i][h] - f * rk[h] for h in range(2)])
        a = new
    return a


def put(ref, a, base=0):
    for i in range(16):
        for h in range(2):
            ref[pl.ds(base + i * 16 + h * 8, 8), :] = a[i][h]


def packed_product(left, right, count):
    out = []
    for i in range(16):
        acc = [row_of(left, i * 16 + k) * right[k] for k in range(count)]
        while len(acc) > 1:
            acc = [acc[q] + acc[q + 1] for q in range(0, len(acc), 2)]
        out.append(acc[0])
    return out


def factor(bmat, emat, ps, qs, gf, left, left2, pivots):
    lane = lax.broadcasted_iota(jnp.int32, (8, 128), 1)
    group = lane // 32
    both = [(i, h) for i in range(16) for h in range(2)]
    two = range(2)

    def by_group(a, b, c, d):
        return jnp.where(group < 2, jnp.where(group == 0, a, b), jnp.where(group == 2, c, d))

    def spread(y):
        r = [y] + [lroll(y, 32 * q) for q in range(1, 4)]
        return [by_group(*(r[(g - c) % 4] for g in range(4))) for c in range(4)]

    def body(m, _):
        d = jnp.left_shift(1, m)
        base = pl.multiple_of(m * 256, 256)

        def ahead(x):
            return pltpu.roll(x, 128 - d, 1)

        def behind(x):
            return pltpu.roll(x, d, 1)

        g = inverted([[mat(bmat, i, h) for h in two] for i in range(16)], pivots)
        u = [[mat(emat, i, h) for h in two] for i in range(16)]
        ut = [[matT(emat, i, h) for h in two] for i in range(16)]
        for i, h in both:
            left[pl.ds(i * 16 + h * 8, 8), :] = jnp.where(group < 2, g[i][h], ahead(g[i][h]))
        for i in range(16):
            left2[pl.ds(i * 16, 8), :] = jnp.where(group < 2, ut[i][0], ut[i][1])
        quarters = [
            spread(y)
            for y in packed_product(left, [by_group(*u[k], *ut[k]) for k in range(16)], 16)
        ]
        q = [y[:2] for y in quarters]
        p = [y[2:] for y in quarters]
        put(ps, p, base)
        put(qs, [[behind(q[i][h]) for h in two] for i in range(16)], base)
        right = [by_group(*p[k], *(ahead(q[k][h]) for h in two)) for k in range(16)]
        first = [spread(y) for y in packed_product(emat, right, 16)]
        right = [by_group(*q[k], *q[k + 8]) for k in range(8)]
        second = []
        for y in packed_product(left2, right, 8):
            y = y + lroll(y, 64)
            z = lroll(y, 32)
            flip = group % 2 == 0
            second.append([jnp.where(flip, y, z), jnp.where(flip, z, y)])
        for i, h in both:
            rows_at = pl.ds(i * 16 + h * 8, 8)
            bmat[rows_at, :] = bmat[rows_at, :] - (first[i][h] + behind(second[i][h]))
            emat[rows_at, :] = -first[i][2 + h]
        return 0

    lax.fori_loop(0, 5, body, 0)
    last = [[mat(bmat, i, h) + (mat(emat, i, h) + matT(emat, i, h)) for h in two] for i in range(16)]
    put(gf, inverted(last, pivots))


def times(ref, base, vec, x):
    vec[pl.ds(0, 8), :], vec[pl.ds(8, 8), :] = x[0], x[1]
    out = []
    for h in range(2):
        terms = [mat(ref, k, h, base) * row_of(vec, k) for k in range(16)]
        while len(terms) > 1:
            terms = [terms[q] + terms[q + 1] for q in range(0, len(terms), 2)]
        out.append(terms[0])
    return out


def ring_solve(r, ps, qs, gf, vecs):
    for m in range(5):
        d = 1 << m
        p = times(ps, m * 256, vecs.at[2 * m], [lroll(r[h], -d) for h in range(2)])
        q = times(qs, m * 256, vecs.at[2 * m + 1], [lroll(r[h], d) for h in range(2)])
        r = [r[h] - (p[h] + q[h]) for h in range(2)]
    return times(gf, 0, vecs.at[10], r)


def conductance_setup(gath, w, ring, mats):
    cond = [gath[0, pl.ds(v, 8, stride=NV), :] * SCALE for v in range(NV)]
    level_weights(cond, 0, *w[0])
    c = coarsened(cond, 1)
    level_weights(c, 1, *w[1])
    c = coarsened(c, 2)
    level_weights(c, 2, *w[2])
    c = coarsened(c, 4)
    sq, sq2, vecs = ring
    bmat, emat, ps, qs, gf, left, left2, pivots = mats
    ring_matrix(to_ring(c, sq, sq2), bmat, emat)
    factor(bmat, emat, ps, qs, gf, left, left2, pivots)


def cycles(gath, w, ring, mats, pot):
    sq, sq2, vecs = ring
    ps, qs, gf = mats[2:5]

    def coarse(r):
        x = ring_solve(to_ring(r, sq, sq2), ps, qs, gf, vecs)
        return from_ring(x, sq, sq2, vecs.at[11])

    def body(_, carry):
        source = [gath[1, pl.ds(v, 8, stride=NV), :] * SCALE for v in range(NV)]
        x = vcycle(0, source, [pot[v] for v in range(NV)], w, coarse)
        for v in range(NV):
            pot[v] = x[v]
        return carry

    for v in range(NV):
        pot[v] = jnp.zeros((8, 128), F32)
    lax.fori_loop(0, CYCLES, body, 0)


def stencil(pot, west, east):
    lane = lax.broadcasted_iota(jnp.int32, (8, 128), 1)
    low, high = lane == 0, lane == 127

    def slope(q):
        return jnp.where(high, 0.0, lroll(q, -1)) - jnp.where(low, 0.0, lroll(q, 1))

    uw = CAP * jnp.tanh(-0.25 * slope(west + pot))
    ue = CAP * jnp.tanh(-0.25 * slope(pot + east))
    r = east - west
    us = jnp.where(low, 0.0, CAP * jnp.tanh(0.25 * (lroll(r, 1) + r)))
    un = jnp.where(high, 0.0, lroll(us, -1))
    pos = [jnp.maximum(u, 0.0) for u in (uw, ue, us, un)]
    neg = [jnp.minimum(u, 0.0) for u in (uw, ue, us, un)]
    centre = 1.0 - (pos[1] - neg[0]) - (pos[3] - neg[2])
    return centre, pos[0], -neg[1], pos[2], -neg[3]


def dynamo_kernel(
    nt, nl, ped_hbm, wind_hbm, cour_hbm, dens_hbm,
    coef, pot_own, ent, ent_l, ent_r, dens, halo, atab, btab,
    ped, wind, cour, part, parts, gath, bsend, brecv, psend,
    wl0, ws0, wn0, kk0, dd0, wl1, ws1, wn1, kk1, wl2, ws2, wn2, kk2,
    sq, sq2, bmat, emat, ps, qs, gf, left, left2, pivots, vecs, pot, whole,
    s_ld, s_t, r_t, s_l, r_l, s_h, r_h, s_b, r_b, s_p, r_p, s_e, r_e, line,
):
    ns, pts = dens.shape[:2]
    t, l = lax.axis_index("tube"), lax.axis_index("lon")
    loads = [
        pltpu.make_async_copy(src, dst, s_ld.at[k])
        for k, (src, dst) in enumerate(
            ((ped_hbm, ped), (wind_hbm, wind), (cour_hbm, cour), (dens_hbm, dens))
        )
    ]
    for c in loads:
        c.start()

    far_t = sorted(range(1, nt), key=lambda o: -min(o, nt - o))
    far_l = sorted(range(1, nl), key=lambda o: -min(o // 2 % 4, 4 - o // 2 % 4) - min(o // 8, 4 - o // 8))
    beside = l + 1 - 2 * lax.rem(l, 2)
    x_line = [l - lax.rem(l, 8) + lax.rem(lax.rem(l, 8) + 2 * o, 8) for o in range(1, 4)]
    y_line = [lax.rem(c + 8 * o, nl) for c in (l, beside) for o in range(1, nl // 8)]
    next_chip = lax.rem(l + 2 * lax.rem(l, 2) - 1 + nl, nl)
    across_lon = y_line + x_line + [beside, next_chip]
    greeted = [(lax.rem(t + o, nt), l) for o in far_t] + [(t, c) for c in across_lon]
    barrier = pltpu.get_barrier_semaphore()
    for to in greeted:
        pl.semaphore_signal(barrier, inc=1, device_id=to, device_id_type=MESH)

    loads[0].wait()
    loads[1].wait()
    csum = [ped[k] for k in range(4)]
    ssum = [ped[k] * wind[k] for k in range(4)]
    for p in range(4, pts):
        csum[p % 4] = csum[p % 4] + ped[p]
        ssum[p % 4] = ssum[p % 4] + ped[p] * wind[p]
    part[0] = (csum[0] + csum[1]) + (csum[2] + csum[3])
    part[1] = (ssum[0] + ssum[1]) + (ssum[2] + ssum[3])

    def remote(src, dst, ssem, rsem, to):
        c = pltpu.make_async_remote_copy(
            src_ref=src, dst_ref=dst, send_sem=ssem, recv_sem=rsem,
            device_id=to, device_id_type=MESH,
        )
        c.start()
        return c

    pl.semaphore_wait(barrier, len(greeted))
    for c in x_line:
        pl.semaphore_signal(line, inc=1, device_id=(t, c), device_id_type=MESH)
    along = []
    for k in range(2):
        for o in far_t:
            to = (lax.rem(t + o, nt), l)
            along.append(remote(part.at[k], parts.at[k, o], s_t.at[k, o], r_t.at[k, o], to))

    right, left_l = lax.rem(l + 1, nl), lax.rem(l + nl - 1, nl)
    h0 = remote(
        dens_hbm.at[:, :, pl.ds(7, 1), :], halo.at[:, :, pl.ds(0, 1), :], s_h.at[0], r_h.at[0], (t, right)
    )
    h1 = remote(
        dens_hbm.at[:, :, pl.ds(0, 1), :], halo.at[:, :, pl.ds(7, 1), :], s_h.at[1], r_h.at[1], (t, left_l)
    )

    loads[2].wait()
    coefficient_tables(cour, atab, btab)
    loads[3].wait()

    def step(p, carry):
        out = []
        for s in range(ns):
            x, m = carry[s]
            a, b = row_of(atab, p * 8 + s), row_of(btab, p * 8 + s)
            out.append((a * x + b * dens[s, p], a * m))
        return tuple(out)

    zero, one = jnp.zeros((8, 128), F32), jnp.ones((8, 128), F32)
    ends = lax.fori_loop(0, pts, step, tuple((zero, one) for _ in range(ns)))
    for s in range(ns):
        bsend[s, 0] = ends[s][0]
        bsend[s, 1] = ends[s][1]

    mine = (t * ns + nt - 1) // nt
    owner_of = [(s * nt) // ns for s in range(ns)]
    is_owner = jnp.logical_and(mine < ns, (mine * nt) // ns == t)
    for s in range(ns):

        @pl.when(t != owner_of[s])
        def _():
            o = lax.rem(t - owner_of[s] + nt, nt)
            remote(bsend.at[s], brecv.at[o], s_b.at[s], r_b.at[o], (owner_of[s], l))

    across = []
    for k in range(2):
        parts[k, 0] = part[k]
        for c in along[k * (nt - 1) : (k + 1) * (nt - 1)]:
            c.wait_recv()
        total = [parts[k, o] for o in range(nt)]
        while len(total) > 1:
            total = [total[q] + total[q + 1] for q in range(0, len(total), 2)]
        block = pl.ds(pl.multiple_of(l * 8, 8), 8)
        gath[k, block, :] = total[0]
        if k == 0:
            pl.semaphore_wait(line, len(x_line))
        for o in far_l:
            to = (t, lax.rem(l + o, nl))
            at = gath.at[k, block, :]
            across.append(remote(at, at, s_l.at[k, o], r_l.at[k, o], to))

    @pl.when(is_owner)
    def _():
        brecv[0] = bsend[mine]
        for o in range(1, nt):
            pltpu.make_async_copy(brecv.at[o], brecv.at[o], r_b.at[o]).wait()
        x = zero
        for k in range(nt):
            psend[k] = x
            o = lax.rem(k - t + nt, nt)
            x = brecv[o, 1] * x + brecv[o, 0]
        ent[mine] = psend[t]
        for o in far_t:
            to = lax.rem(t + o, nt)
            remote(psend.at[to], ent.at[mine], s_p.at[o], r_p.at[mine], (to, l))

    for c in across[: nl - 1]:
        c.wait_recv()

    w = [(wl0, ws0, wn0, kk0, dd0), (wl1, ws1, wn1, kk1, None), (wl2, ws2, wn2, kk2, None)]
    ring, mats = (sq, sq2, vecs), (bmat, emat, ps, qs, gf, left, left2, pivots)
    conductance_setup(gath, w, ring, mats)

    for s in range(ns):

        @pl.when(t != owner_of[s])
        def _():
            pltpu.make_async_copy(ent.at[s], ent.at[s], r_p.at[s]).wait()

    e0 = remote(ent, ent_l, s_e.at[0], r_e.at[0], (t, right))
    e1 = remote(ent, ent_r, s_e.at[1], r_e.at[1], (t, left_l))

    for c in across[nl - 1 :]:
        c.wait_recv()
    cycles(gath, w, ring, mats, pot)
    for v in range(NV):
        whole[pl.ds(v, 8, stride=NV), :] = pot[v]
    own = whole[pl.ds(pl.multiple_of(l * 8, 8), 8), :]
    sub = lax.broadcasted_iota(jnp.int32, (8, 128), 0)
    west = jnp.where(sub == 0, row_of(whole, lax.rem(l * 8 + 255, 256)), pltpu.roll(own, 1, 0))
    east = jnp.where(sub == 7, row_of(whole, lax.rem(l * 8 + 8, 256)), pltpu.roll(own, 7, 0))
    pot_own[...] = own
    for k, c in enumerate(stencil(own, west, east)):
        coef[k] = c

    for c in along + across:
        c.wait_send()
    for s in range(ns):

        @pl.when(t != owner_of[s])
        def _():
            pltpu.make_async_copy(bsend.at[s], bsend.at[s], s_b.at[s]).wait()

    @pl.when(is_owner)
    def _():
        for o in range(1, nt):
            pltpu.make_async_copy(psend.at[0], psend.at[0], s_p.at[o]).wait()

    for c in (h0, h1, e0, e1):
        c.wait()


VM = pl.BlockSpec(memory_space=pltpu.VMEM)
HBM = pl.BlockSpec(memory_space=pltpu.HBM)


def tiles(*n):
    return pltpu.VMEM((*n, 8, 128), F32)


def rows(n):
    return pltpu.VMEM((n, 128), F32)


def dynamo(mesh, density, pedersen, wind, courant):
    nt, nl = mesh.shape["tube"], mesh.shape["lon"]
    ns, pts = density.shape[:2]
    dma = pltpu.SemaphoreType.DMA
    state = jax.ShapeDtypeStruct((ns, 8, 128), F32)
    table = jax.ShapeDtypeStruct((pts * 8, 128), F32)
    levels = [tiles(33)] + [tiles(32)] * 4 + [tiles(17)] + [tiles(16)] * 3 + [tiles(9)] + [tiles(8)] * 3
    return pl.pallas_call(
        functools.partial(dynamo_kernel, nt, nl),
        out_shape=(
            jax.ShapeDtypeStruct((5, 8, 128), F32),
            jax.ShapeDtypeStruct((8, 128), F32),
            state, state, state,
            jax.ShapeDtypeStruct(density.shape, F32),
            jax.ShapeDtypeStruct(density.shape, F32),
            table, table,
        ),
        in_specs=[HBM] * 4,
        out_specs=(VM,) * 9,
        scratch_shapes=[
            tiles(pts), tiles(pts), pltpu.VMEM((ns, pts), F32),
            tiles(2), tiles(2, nt), pltpu.VMEM((2, 8 * nl, 128), F32),
            tiles(ns, 2), tiles(nt, 2), tiles(nt),
        ]
        + levels
        + [rows(128), rows(128), rows(256), rows(256), rows(5 * 256), rows(5 * 256), rows(256)]
        + [rows(256), rows(256), rows(256), pltpu.VMEM((12, 16, 128), F32), tiles(NV), rows(256)]
        + [
            dma((4,)), dma((2, nt)), dma((2, nt)), dma((2, nl)), dma((2, nl)), dma((2,)), dma((2,)),
            dma((ns,)), dma((nt,)), dma((nt,)), dma((ns,)), dma((2,)), dma((2,)),
            pltpu.SemaphoreType.REGULAR,
        ],
        compiler_params=pltpu.CompilerParams(
            collective_id=0, has_side_effects=True, vmem_limit_bytes=40 * 2**20
        ),
        name="dynamo",
    )(pedersen, wind, courant, density)


def transport_kernel(coef, pot_in, ent, ent_l, ent_r, dens, halo, atab, btab, out_hbm, pot, out, sem):
    ns, pts = out.shape[:2]
    pot[...] = pot_in[...]
    cc, cw, ce, cs, cn = (coef[k] for k in range(5))
    sub = lax.broadcasted_iota(jnp.int32, (8, 128), 0)
    start = []
    for s in range(ns):
        side = jnp.where(sub == 0, pltpu.roll(ent_l[s], 1, 0), pltpu.roll(ent_r[s], 7, 0))
        start.append((ent[s], side))

    def step(p, carry):
        new = []
        for s in range(ns):
            y, side = carry[s]
            a, b = row_of(atab, p * 8 + s), row_of(btab, p * 8 + s)
            y = a * y + b * dens[s, p]
            side = a * side + b * halo[s, p]
            yw = jnp.where(sub == 0, side, pltpu.roll(y, 1, 0))
            ye = jnp.where(sub == 7, side, pltpu.roll(y, 7, 0))
            out[s, p] = (cc * y + (cw * yw + ce * ye)) + (cs * lroll(y, 1) + cn * lroll(y, -1))
            new.append((y, side))
        return tuple(new)

    stores, carry = [], tuple(start)
    for k in range(pts // CHUNK):
        carry = lax.fori_loop(k * CHUNK, (k + 1) * CHUNK, step, carry, unroll=True)
        at = pl.ds(k * CHUNK, CHUNK)
        stores.append(pltpu.make_async_copy(out.at[:, at], out_hbm.at[:, at], sem.at[k]))
        stores[-1].start()
    for c in stores:
        c.wait()


def transport(coef, pot, ent, ent_l, ent_r, density, halo, atab, btab):
    return pl.pallas_call(
        transport_kernel,
        out_shape=(
            jax.ShapeDtypeStruct(density.shape, F32),
            jax.ShapeDtypeStruct((8, 128), F32),
        ),
        in_specs=[VM] * 9,
        out_specs=(pl.BlockSpec(memory_space=pl.ANY), VM),
        scratch_shapes=[pltpu.VMEM(density.shape, F32), pltpu.SemaphoreType.DMA((density.shape[1] // CHUNK,))],
        compiler_params=pltpu.CompilerParams(vmem_limit_bytes=24 * 2**20),
        name="transport",
    )(coef, pot, ent, ent_l, ent_r, density, halo, atab, btab)


def solution(mesh):
    def on_device(density, pedersen, wind, courant):
        args = (density, pedersen, wind, courant)
        args = (pltpu.with_memory_space_constraint(x, pltpu.HBM) for x in args)
        return transport(*dynamo(mesh, *args))

    return jax.shard_map(
        on_device,
        mesh=mesh,
        in_specs=(
            P(None, "tube", "lon", None),
            P("tube", "lon", None),
            P("tube", "lon", None),
            P(None, "tube"),
        ),
        out_specs=(P(None, "tube", "lon", None), P("lon", None)),
        check_vma=False,
    )
```

```python
import functools

import jax
import jax.numpy as jnp
from jax import lax
from jax.experimental import pallas as pl
from jax.experimental.pallas import tpu as pltpu
from jax.sharding import PartitionSpec as P

F32 = jnp.float32
SCREENING = 0.005
CAP = 0.2
NV = 32
CYCLES = 3
SPLIT = 2
CHUNK = 8
SCALE = 1.0 / 512.0
MESH = pl.DeviceIdType.MESH


def row_of(ref, r):
    return jnp.broadcast_to(ref[pl.ds(r, 1), :], (8, 128))


def coefficient_tables(cour, atab, btab):
    c = cour[...]
    inv = 1.0 / (1.0 + c)
    keep = c * inv
    ns, pts = c.shape
    for p in range(pts):
        atab[pl.ds(p * 8, ns), :] = jnp.broadcast_to(keep[:, p : p + 1], (ns, 128))
        btab[pl.ds(p * 8, ns), :] = jnp.broadcast_to(inv[:, p : p + 1], (ns, 128))


def lroll(x, shift):
    return pltpu.roll(x, shift % 128, x.ndim - 1)


def before(x):
    return [pltpu.roll(x[-1], 1, 0)] + x[:-1]


def after(x):
    return x[1:] + [pltpu.roll(x[0], 7, 0)]


def level_weights(cond, level, wl, ws, wn, kk, dd):
    half, step, n = 0.5 * 0.25**level, 2**level, len(cond)
    lane = lax.broadcasted_iota(jnp.int32, (8, 128), 1)
    lo, hi = lane >= step, lane < 128 - step
    west = [half * (a + b) for a, b in zip(before(cond), cond)]
    west.append(pltpu.roll(west[0], 7, 0))
    for v in range(n + 1):
        wl[v] = west[v]
    for v in range(n):
        c = cond[v]
        south = half * (c + jnp.where(lo, lroll(c, step), 0.0))
        north = half * (c + jnp.where(hi, lroll(c, -step), 0.0))
        ws[v] = jnp.where(lo, south, 0.0)
        wn[v] = jnp.where(hi, north, 0.0)
        diagonal = (west[v] + west[v + 1]) + (south + north) + SCREENING
        kk[v] = 0.8 / diagonal
        if dd is not None:
            dd[v] = diagonal


def coarsened(x, step):
    lane = lax.broadcasted_iota(jnp.int32, (8, 128), 1)
    low = (lane // step) % 2 == 0
    out = []
    for v in range(0, len(x), 2):
        y = x[v] + x[v + 1]
        out.append(0.25 * (y + jnp.where(low, lroll(y, -step), lroll(y, step))))
    return out


def pulled(x, w, level):
    wl, ws, wn = w[:3]
    step, b, a = 2**level, before(x), after(x)
    return [
        (wl[v] * b[v] + wl[v + 1] * a[v])
        + (ws[v] * lroll(x[v], step) + wn[v] * lroll(x[v], -step))
        for v in range(len(x))
    ]


def vcycle(level, rhs, start, w, coarse):
    if level == len(w):
        return coarse(rhs)
    n = len(rhs)
    kk = w[level][3]
    if start is None:
        x = [kk[v] * rhs[v] for v in range(n)]
        e = [0.2 * r + p for r, p in zip(rhs, pulled(x, w[level], level))]
    else:
        dd = w[level][4]
        p = pulled(start, w[level], level)
        x = [0.2 * start[v] + kk[v] * (rhs[v] + p[v]) for v in range(n)]
        p = pulled(x, w[level], level)
        e = [(rhs[v] - dd[v] * x[v]) + p[v] for v in range(n)]
    fix = vcycle(level + 1, coarsened(e, 2**level), None, w, coarse)
    x = [x[v] + fix[v // 2] for v in range(n)]
    p = pulled(x, w[level], level)
    return [0.2 * x[v] + kk[v] * (rhs[v] + p[v]) for v in range(n)]


def to_ring(x, sq, sq2):
    for v in range(4):
        for rep in range(4):
            sq[pl.ds(rep * 32 + v, 8, stride=4), :] = x[v]
    sq2[...] = sq[...].T
    return [sq2[pl.ds(0, 8, stride=8), :], sq2[pl.ds(64, 8, stride=8), :]]


def from_ring(x, sq, sq2, vec):
    vec[pl.ds(0, 8), :], vec[pl.ds(8, 8), :] = x[0], x[1]
    for j in range(16):
        sq[pl.ds(j * 8, 8), :] = row_of(vec, j)
    sq2[...] = sq[...].T
    return [sq2[pl.ds(v, 8, stride=4), :] for v in range(4)]


def ring_matrix(c, bmat, emat):
    sub = [lax.broadcasted_iota(jnp.int32, (8, 128), 0) + 8 * h for h in range(2)]
    half = 0.5 * 0.25**3
    east = [half * (c[h] + lroll(c[h], -1)) for h in range(2)]
    up = [pltpu.roll(c[h], 1, 0) for h in range(2)]
    dn = [pltpu.roll(c[h], 7, 0) for h in range(2)]
    first, last = sub[0] % 8 == 0, sub[0] % 8 == 7
    below = [jnp.where(first, 0.0, up[0]), jnp.where(first, up[0], up[1])]
    above = [jnp.where(last, dn[1], dn[0]), jnp.where(last, 0.0, dn[1])]
    south = [half * (c[h] + below[h]) for h in range(2)]
    north = [half * (c[h] + above[h]) for h in range(2)]
    for i in range(16):
        for h in range(2):
            j = sub[h]
            diagonal = (east[h] + lroll(east[h], 1)) + (south[h] + north[h]) + SCREENING
            value = jnp.where(j == i, diagonal, 0.0)
            value = jnp.where(j == i + 1, -south[h], value)
            value = jnp.where(j == i - 1, -north[h], value)
            bmat[pl.ds(i * 16 + h * 8, 8), :] = value
            emat[pl.ds(i * 16 + h * 8, 8), :] = jnp.where(j == i, -east[h], 0.0)


def mat(ref, i, h, base=0):
    return ref[pl.ds(base + i * 16 + h * 8, 8), :]


def matT(ref, i, h, base=0):
    return ref[pl.ds(base + h * 128 + i, 8, stride=16), :]


def inverted(a, pivots):
    sub = [lax.broadcasted_iota(jnp.int32, (8, 128), 0) + 8 * h for h in range(2)]
    for k in range(16):
        hk = k // 8
        base = k * 16
        for h in range(2):
            pivots[pl.ds(base + h * 8, 8), :] = a[k][h]
        p = 1.0 / row_of(pivots, base + k)
        scaled = [a[k][h] * p for h in range(2)]
        rk = list(scaled)
        rk[hk] = jnp.where(sub[hk] == k, 1.0 + p, rk[hk])
        new = []
        for i in range(16):
            if i == k:
                fin = list(scaled)
                fin[hk] = jnp.where(sub[hk] == k, p, fin[hk])
                new.append(fin)
                continue
            f = row_of(pivots, base + i)
            if i < k:
                f = -f
            new.append([a[i][h] - f * rk[h] for h in range(2)])
        a = new
    return a


def put(ref, a, base=0):
    for i in range(16):
        for h in range(2):
            ref[pl.ds(base + i * 16 + h * 8, 8), :] = a[i][h]


def packed_product(left, right, count):
    out = []
    for i in range(16):
        acc = [row_of(left, i * 16 + k) * right[k] for k in range(count)]
        while len(acc) > 1:
            acc = [acc[q] + acc[q + 1] for q in range(0, len(acc), 2)]
        out.append(acc[0])
    return out


def factor(bmat, emat, ps, qs, gf, left, left2, pivots):
    lane = lax.broadcasted_iota(jnp.int32, (8, 128), 1)
    group = lane // 32
    both = [(i, h) for i in range(16) for h in range(2)]
    two = range(2)

    def by_group(a, b, c, d):
        return jnp.where(group < 2, jnp.where(group == 0, a, b), jnp.where(group == 2, c, d))

    def spread(y):
        r = [y] + [lroll(y, 32 * q) for q in range(1, 4)]
        return [by_group(*(r[(g - c) % 4] for g in range(4))) for c in range(4)]

    def body(m, _):
        d = jnp.left_shift(1, m)
        base = pl.multiple_of(m * 256, 256)

        def ahead(x):
            return pltpu.roll(x, 128 - d, 1)

        def behind(x):
            return pltpu.roll(x, d, 1)

        g = inverted([[mat(bmat, i, h) for h in two] for i in range(16)], pivots)
        u = [[mat(emat, i, h) for h in two] for i in range(16)]
        ut = [[matT(emat, i, h) for h in two] for i in range(16)]
        for i, h in both:
            left[pl.ds(i * 16 + h * 8, 8), :] = jnp.where(group < 2, g[i][h], ahead(g[i][h]))
        for i in range(16):
            left2[pl.ds(i * 16, 8), :] = jnp.where(group < 2, ut[i][0], ut[i][1])
        quarters = [
            spread(y)
            for y in packed_product(left, [by_group(*u[k], *ut[k]) for k in range(16)], 16)
        ]
        q = [y[:2] for y in quarters]
        p = [y[2:] for y in quarters]
        put(ps, p, base)
        put(qs, [[behind(q[i][h]) for h in two] for i in range(16)], base)
        right = [by_group(*p[k], *(ahead(q[k][h]) for h in two)) for k in range(16)]
        first = [spread(y) for y in packed_product(emat, right, 16)]
        right = [by_group(*q[k], *q[k + 8]) for k in range(8)]
        second = []
        for y in packed_product(left2, right, 8):
            y = y + lroll(y, 64)
            z = lroll(y, 32)
            flip = group % 2 == 0
            second.append([jnp.where(flip, y, z), jnp.where(flip, z, y)])
        for i, h in both:
            rows_at = pl.ds(i * 16 + h * 8, 8)
            bmat[rows_at, :] = bmat[rows_at, :] - (first[i][h] + behind(second[i][h]))
            emat[rows_at, :] = -first[i][2 + h]
        return 0

    lax.fori_loop(0, 5, body, 0)
    last = [[mat(bmat, i, h) + (mat(emat, i, h) + matT(emat, i, h)) for h in two] for i in range(16)]
    put(gf, inverted(last, pivots))


def times(ref, base, vec, x):
    vec[pl.ds(0, 8), :], vec[pl.ds(8, 8), :] = x[0], x[1]
    out = []
    for h in range(2):
        terms = [mat(ref, k, h, base) * row_of(vec, k) for k in range(16)]
        while len(terms) > 1:
            terms = [terms[q] + terms[q + 1] for q in range(0, len(terms), 2)]
        out.append(terms[0])
    return out


def ring_solve(r, ps, qs, gf, vecs):
    for m in range(5):
        d = 1 << m
        p = times(ps, m * 256, vecs.at[2 * m], [lroll(r[h], -d) for h in range(2)])
        q = times(qs, m * 256, vecs.at[2 * m + 1], [lroll(r[h], d) for h in range(2)])
        r = [r[h] - (p[h] + q[h]) for h in range(2)]
    return times(gf, 0, vecs.at[10], r)


def coarse_setup(coarse, ring, mats):
    sq, sq2, vecs = ring
    bmat, emat, ps, qs, gf, left, left2, pivots = mats
    lane = lax.broadcasted_iota(jnp.int32, (8, 128), 1)
    for v in range(4):
        y = coarse[pl.ds(v * 8, 8), :] * (SCALE / 64.0)
        for step in (1, 2, 4):
            y = y + jnp.where((lane // step) % 2 == 0, lroll(y, -step), lroll(y, step))
        for rep in range(4):
            sq[pl.ds(rep * 32 + v * 8, 8), :] = y
    sq2[...] = sq[...].T
    ring_matrix([sq2[pl.ds(64 * h, 8, stride=8), :] for h in range(2)], bmat, emat)
    factor(bmat, emat, ps, qs, gf, left, left2, pivots)


def conductance_setup(gath, w):
    cond = [gath[0, pl.ds(v, 8, stride=NV), :] * SCALE for v in range(NV)]
    level_weights(cond, 0, *w[0])
    c = coarsened(cond, 1)
    level_weights(c, 1, *w[1])
    level_weights(coarsened(c, 2), 2, *w[2])


def cycles(gath, w, ring, mats, pot):
    sq, sq2, vecs = ring
    ps, qs, gf = mats[2:5]

    def coarse(r):
        x = ring_solve(to_ring(r, sq, sq2), ps, qs, gf, vecs)
        return from_ring(x, sq, sq2, vecs.at[11])

    def sweep(start):
        source = [gath[1, pl.ds(v, 8, stride=NV), :] * SCALE for v in range(NV)]
        x = vcycle(0, source, start, w, coarse)
        for v in range(NV):
            pot[v] = x[v]

    def body(_, carry):
        sweep([pot[v] for v in range(NV)])
        return carry

    sweep(None)
    lax.fori_loop(1, CYCLES, body, 0)


def stencil(pot, west, east):
    lane = lax.broadcasted_iota(jnp.int32, (8, 128), 1)
    low, high = lane == 0, lane == 127

    def slope(q):
        return jnp.where(high, 0.0, lroll(q, -1)) - jnp.where(low, 0.0, lroll(q, 1))

    uw = CAP * jnp.tanh(-0.25 * slope(west + pot))
    ue = CAP * jnp.tanh(-0.25 * slope(pot + east))
    r = east - west
    us = jnp.where(low, 0.0, CAP * jnp.tanh(0.25 * (lroll(r, 1) + r)))
    un = jnp.where(high, 0.0, lroll(us, -1))
    pos = [jnp.maximum(u, 0.0) for u in (uw, ue, us, un)]
    neg = [jnp.minimum(u, 0.0) for u in (uw, ue, us, un)]
    centre = 1.0 - (pos[1] - neg[0]) - (pos[3] - neg[2])
    return centre, pos[0], -neg[1], pos[2], -neg[3]


def dynamo_kernel(
    nt, nl, ped_hbm, wind_hbm, cour_hbm, dens_hbm,
    coef, pot_own, ent, sides, dens, halo, atab, btab,
    ped, wind, cour, part, parts, gath, crow, crows, coarse, rows32, bsend, brecv, psend,
    wl0, ws0, wn0, kk0, dd0, wl1, ws1, wn1, kk1, wl2, ws2, wn2, kk2,
    sq, sq2, bmat, emat, ps, qs, gf, left, left2, pivots, vecs, pot, whole,
    s_ld, s_t, r_t, s_l, r_l, s_h, r_h, s_b, r_b, s_p, r_p, s_e, r_e, s_c, r_c, line,
):
    ns, pts = dens.shape[:2]
    t, l = lax.axis_index("tube"), lax.axis_index("lon")
    loads = [
        pltpu.make_async_copy(src, dst, s_ld.at[k])
        for k, (src, dst) in enumerate(
            ((ped_hbm, ped), (wind_hbm, wind), (cour_hbm, cour), (dens_hbm, dens))
        )
    ]
    for c in loads:
        c.start()

    far_t = sorted(range(1, nt), key=lambda o: -min(o, nt - o))
    far_l = sorted(range(1, nl), key=lambda o: -min(o // 2 % 4, 4 - o // 2 % 4) - min(o // 8, 4 - o // 8))
    beside = l + 1 - 2 * lax.rem(l, 2)
    x_line = [l - lax.rem(l, 8) + lax.rem(lax.rem(l, 8) + 2 * o, 8) for o in range(1, 4)]
    y_line = [lax.rem(c + 8 * o, nl) for c in (l, beside) for o in range(1, nl // 8)]
    next_chip = lax.rem(l + 2 * lax.rem(l, 2) - 1 + nl, nl)
    across_lon = y_line + x_line + [beside, next_chip]
    greeted = [(lax.rem(t + o, nt), l) for o in far_t] + [(t, c) for c in across_lon]
    barrier = pltpu.get_barrier_semaphore()
    for to in greeted:
        pl.semaphore_signal(barrier, inc=1, device_id=to, device_id_type=MESH)

    loads[0].wait()
    loads[1].wait()
    csum = [ped[k] for k in range(4)]
    ssum = [ped[k] * wind[k] for k in range(4)]
    for p in range(4, pts):
        csum[p % 4] = csum[p % 4] + ped[p]
        ssum[p % 4] = ssum[p % 4] + ped[p] * wind[p]
    part[0] = total = (csum[0] + csum[1]) + (csum[2] + csum[3])
    part[1] = (ssum[0] + ssum[1]) + (ssum[2] + ssum[3])

    def remote(src, dst, ssem, rsem, to):
        c = pltpu.make_async_remote_copy(
            src_ref=src, dst_ref=dst, send_sem=ssem, recv_sem=rsem,
            device_id=to, device_id_type=MESH,
        )
        c.start()
        return c

    def settle(ref, sem):
        pltpu.make_async_copy(ref, ref, sem).wait()

    pl.semaphore_wait(barrier, len(greeted))
    for c in x_line:
        pl.semaphore_signal(line, inc=1, device_id=(t, c), device_id_type=MESH)
    crow[...] = jnp.sum(total, axis=0, keepdims=True)
    for o in far_t:
        to = (lax.rem(t + o, nt), l)
        remote(crow, crows.at[o], s_c.at[0], r_c.at[0], to)
    fields = [pl.ds(k * (2 // SPLIT), 2 // SPLIT) for k in range(SPLIT)]
    for k in range(SPLIT):
        for o in far_t:
            to = (lax.rem(t + o, nt), l)
            remote(part.at[fields[k]], parts.at[o, fields[k]], s_t.at[k], r_t.at[k], to)

    right, left_l = lax.rem(l + 1, nl), lax.rem(l + nl - 1, nl)
    h0 = remote(
        dens_hbm.at[:, :, pl.ds(7, 1), :], halo.at[:, :, pl.ds(0, 1), :], s_h.at[0], r_h.at[0], (t, right)
    )
    h1 = remote(
        dens_hbm.at[:, :, pl.ds(0, 1), :], halo.at[:, :, pl.ds(7, 1), :], s_h.at[1], r_h.at[1], (t, left_l)
    )

    loads[2].wait()
    coefficient_tables(cour, atab, btab)
    loads[3].wait()

    def step(p, carry):
        out = []
        for s in range(ns):
            x, m = carry[s]
            a, b = row_of(atab, p * 8 + s), row_of(btab, p * 8 + s)
            out.append((a * x + b * dens[s, p], a * m))
        return tuple(out)

    zero, one = jnp.zeros((8, 128), F32), jnp.ones((8, 128), F32)
    ends = lax.fori_loop(0, pts, step, tuple((zero, one) for _ in range(ns)))
    for s in range(ns):
        bsend[s, 0] = ends[s][0]
        bsend[s, 1] = ends[s][1]

    mine = (t * ns + nt - 1) // nt
    owner_of = [(s * nt) // ns for s in range(ns)]
    is_owner = jnp.logical_and(mine < ns, (mine * nt) // ns == t)
    for s in range(ns):

        @pl.when(t != owner_of[s])
        def _():
            o = lax.rem(t - owner_of[s] + nt, nt)
            remote(bsend.at[s], brecv.at[o], s_b, r_b, (owner_of[s], l))

    others_t, others_l = pl.ds(1, nt - 1), pl.ds(0, (nl - 1) * 8)
    settle(crows.at[others_t], r_c.at[0])
    total = [crow[...]] + [crows[o] for o in range(1, nt)]
    while len(total) > 1:
        total = [total[q] + total[q + 1] for q in range(0, len(total), 2)]
    coarse[l] = total[0]
    pl.semaphore_wait(line, len(x_line))
    for o in far_l:
        to = (t, lax.rem(l + o, nl))
        remote(coarse.at[l], coarse.at[l], s_c.at[1], r_c.at[1], to)
    block = pl.ds(pl.multiple_of(l * 8, 8), 8)
    for k in range(SPLIT):
        settle(parts.at[others_t, fields[k]], r_t.at[k])
        total = [part[fields[k]]] + [parts[o, fields[k]] for o in range(1, nt)]
        while len(total) > 1:
            total = [total[q] + total[q + 1] for q in range(0, len(total), 2)]
        gath[fields[k], block, :] = total[0]
        for o in far_l:
            to = (t, lax.rem(l + o, nl))
            at = gath.at[fields[k], block, :]
            remote(at, at, s_l.at[k], r_l.at[k], to)

    west_row, east_row = pl.ds(0, 1), pl.ds(7, 1)

    @pl.when(is_owner)
    def _():
        brecv[0] = bsend[mine]
        settle(brecv.at[others_t], r_b)
        x = zero
        for k in range(nt):
            psend[k] = x
            o = lax.rem(k - t + nt, nt)
            x = brecv[o, 1] * x + brecv[o, 0]
        ent[mine] = psend[t]
        for o in far_t + [0]:
            to = lax.rem(t + o, nt)
            if o:
                remote(psend.at[to], ent.at[mine], s_p, r_p, (to, l))
            for k, (row, side) in enumerate(((east_row, right), (west_row, left_l))):
                remote(psend.at[to, row], sides.at[mine, west_row if k == 0 else east_row],
                       s_e, r_e, (to, side))

    w = [(wl0, ws0, wn0, kk0, dd0), (wl1, ws1, wn1, kk1, None), (wl2, ws2, wn2, kk2, None)]
    ring, mats = (sq, sq2, vecs), (bmat, emat, ps, qs, gf, left, left2, pivots)
    settle(coarse.at[pl.ds(0, nl - 1)], r_c.at[1])
    for r in range(nl):
        rows32[pl.ds(r, 1), :] = coarse[r]
    coarse_setup(rows32, ring, mats)
    settle(gath.at[fields[0], others_l], r_l.at[0])
    conductance_setup(gath, w)

    for k in range(1, SPLIT):
        settle(gath.at[fields[k], others_l], r_l.at[k])
    cycles(gath, w, ring, mats, pot)
    for v in range(NV):
        whole[pl.ds(v, 8, stride=NV), :] = pot[v]
    own = whole[pl.ds(pl.multiple_of(l * 8, 8), 8), :]
    sub = lax.broadcasted_iota(jnp.int32, (8, 128), 0)
    west = jnp.where(sub == 0, row_of(whole, lax.rem(l * 8 + 255, 256)), pltpu.roll(own, 1, 0))
    east = jnp.where(sub == 7, row_of(whole, lax.rem(l * 8 + 8, 256)), pltpu.roll(own, 7, 0))
    pot_own[...] = own
    for k, c in enumerate(stencil(own, west, east)):
        coef[k] = c

    settle(crows.at[others_t], s_c.at[0])
    settle(coarse.at[pl.ds(0, nl - 1)], s_c.at[1])
    for k in range(SPLIT):
        settle(parts.at[others_t, fields[k]], s_t.at[k])
        settle(gath.at[fields[k], others_l], s_l.at[k])

    @pl.when(is_owner)
    def _():
        settle(bsend.at[pl.ds(0, ns - 1)], s_b)
        settle(ent.at[pl.ds(0, ns - 1)], r_p)
        settle(psend.at[others_t], s_p)
        settle(psend.at[pl.ds(0, nt // 4)], s_e)

    @pl.when(jnp.logical_not(is_owner))
    def _():
        settle(bsend, s_b)
        settle(ent, r_p)

    settle(sides.at[:, pl.ds(0, 2), :], r_e)
    for c in (h0, h1):
        c.wait()


VM = pl.BlockSpec(memory_space=pltpu.VMEM)
HBM = pl.BlockSpec(memory_space=pltpu.HBM)


def tiles(*n):
    return pltpu.VMEM((*n, 8, 128), F32)


def rows(n):
    return pltpu.VMEM((n, 128), F32)


def dynamo(mesh, density, pedersen, wind, courant):
    nt, nl = mesh.shape["tube"], mesh.shape["lon"]
    ns, pts = density.shape[:2]
    dma = pltpu.SemaphoreType.DMA
    state = jax.ShapeDtypeStruct((ns, 8, 128), F32)
    table = jax.ShapeDtypeStruct((pts * 8, 128), F32)
    levels = [tiles(33)] + [tiles(32)] * 4 + [tiles(17)] + [tiles(16)] * 3 + [tiles(9)] + [tiles(8)] * 3
    return pl.pallas_call(
        functools.partial(dynamo_kernel, nt, nl),
        out_shape=(
            jax.ShapeDtypeStruct((5, 8, 128), F32),
            jax.ShapeDtypeStruct((8, 128), F32),
            state, state,
            jax.ShapeDtypeStruct(density.shape, F32),
            jax.ShapeDtypeStruct(density.shape, F32),
            table, table,
        ),
        in_specs=[HBM] * 4,
        out_specs=(VM,) * 8,
        scratch_shapes=[
            tiles(pts), tiles(pts), pltpu.VMEM((ns, pts), F32),
            tiles(2), tiles(nt, 2), pltpu.VMEM((2, 8 * nl, 128), F32),
            rows(1), pltpu.VMEM((nt, 1, 128), F32), pltpu.VMEM((nl, 1, 128), F32), rows(nl),
            tiles(ns, 2), tiles(nt, 2), tiles(nt),
        ]
        + levels
        + [rows(128), rows(128), rows(256), rows(256), rows(5 * 256), rows(5 * 256), rows(256)]
        + [rows(256), rows(256), rows(256), pltpu.VMEM((12, 16, 128), F32), tiles(NV), rows(256)]
        + [
            dma((4,)), dma((2,)), dma((2,)), dma((2,)), dma((2,)), dma((2,)), dma((2,)),
            dma, dma, dma, dma, dma, dma, dma((2,)), dma((2,)), pltpu.SemaphoreType.REGULAR,
        ],
        compiler_params=pltpu.CompilerParams(
            collective_id=0, has_side_effects=True, vmem_limit_bytes=40 * 2**20
        ),
        name="dynamo",
    )(pedersen, wind, courant, density)


def transport_kernel(coef, pot_in, ent, sides, dens, halo, atab, btab, out_hbm, pot, out, sem):
    ns, pts = out.shape[:2]
    pot[...] = pot_in[...]
    cc, cw, ce, cs, cn = (coef[k] for k in range(5))
    sub = lax.broadcasted_iota(jnp.int32, (8, 128), 0)
    start = [(ent[s], sides[s]) for s in range(ns)]

    def step(p, carry):
        new = []
        for s in range(ns):
            y, side = carry[s]
            a, b = row_of(atab, p * 8 + s), row_of(btab, p * 8 + s)
            y = a * y + b * dens[s, p]
            side = a * side + b * halo[s, p]
            yw = jnp.where(sub == 0, side, pltpu.roll(y, 1, 0))
            ye = jnp.where(sub == 7, side, pltpu.roll(y, 7, 0))
            out[s, p] = (cc * y + (cw * yw + ce * ye)) + (cs * lroll(y, 1) + cn * lroll(y, -1))
            new.append((y, side))
        return tuple(new)

    stores, carry = [], tuple(start)
    for k in range(pts // CHUNK):
        carry = lax.fori_loop(k * CHUNK, (k + 1) * CHUNK, step, carry, unroll=True)
        at = pl.ds(k * CHUNK, CHUNK)
        stores.append(pltpu.make_async_copy(out.at[:, at], out_hbm.at[:, at], sem.at[k]))
        stores[-1].start()
    for c in stores:
        c.wait()


def transport(coef, pot, ent, sides, density, halo, atab, btab):
    return pl.pallas_call(
        transport_kernel,
        out_shape=(
            jax.ShapeDtypeStruct(density.shape, F32),
            jax.ShapeDtypeStruct((8, 128), F32),
        ),
        in_specs=[VM] * 8,
        out_specs=(pl.BlockSpec(memory_space=pl.ANY), VM),
        scratch_shapes=[pltpu.VMEM(density.shape, F32), pltpu.SemaphoreType.DMA((density.shape[1] // CHUNK,))],
        compiler_params=pltpu.CompilerParams(vmem_limit_bytes=24 * 2**20),
        name="transport",
    )(coef, pot, ent, sides, density, halo, atab, btab)


def solution(mesh):
    def on_device(density, pedersen, wind, courant):
        args = (density, pedersen, wind, courant)
        args = (pltpu.with_memory_space_constraint(x, pltpu.HBM) for x in args)
        return transport(*dynamo(mesh, *args))

    return jax.shard_map(
        on_device,
        mesh=mesh,
        in_specs=(
            P(None, "tube", "lon", None),
            P("tube", "lon", None),
            P("tube", "lon", None),
            P(None, "tube"),
        ),
        out_specs=(P(None, "tube", "lon", None), P("lon", None)),
        check_vma=False,
    )
```

```python
import functools

import jax
import jax.numpy as jnp
from jax import lax
from jax.experimental import pallas as pl
from jax.experimental.pallas import tpu as pltpu
from jax.sharding import PartitionSpec as P

F32 = jnp.float32
SCREENING = 0.005
CAP = 0.2
NV = 32
CYCLES = 3
SPLIT = 2
CHUNK = 8
SCALE = 1.0 / 512.0
MESH = pl.DeviceIdType.MESH


def row_of(ref, r):
    return jnp.broadcast_to(ref[pl.ds(r, 1), :], (8, 128))


def coefficient_tables(cour, atab, btab):
    c = cour[...]
    inv = 1.0 / (1.0 + c)
    keep = c * inv
    ns, pts = c.shape
    for p in range(pts):
        atab[pl.ds(p * 8, ns), :] = jnp.broadcast_to(keep[:, p : p + 1], (ns, 128))
        btab[pl.ds(p * 8, ns), :] = jnp.broadcast_to(inv[:, p : p + 1], (ns, 128))


def lroll(x, shift):
    return pltpu.roll(x, shift % 128, x.ndim - 1)


def before(x):
    return [pltpu.roll(x[-1], 1, 0)] + x[:-1]


def after(x):
    return x[1:] + [pltpu.roll(x[0], 7, 0)]


def level_weights(cond, level, wl, ws, wn, kk, dd):
    half, step, n = 0.5 * 0.25**level, 2**level, len(cond)
    lane = lax.broadcasted_iota(jnp.int32, (8, 128), 1)
    lo, hi = lane >= step, lane < 128 - step
    west = [half * (a + b) for a, b in zip(before(cond), cond)]
    west.append(pltpu.roll(west[0], 7, 0))
    for v in range(n + 1):
        wl[v] = west[v]
    for v in range(n):
        c = cond[v]
        south = half * (c + jnp.where(lo, lroll(c, step), 0.0))
        north = half * (c + jnp.where(hi, lroll(c, -step), 0.0))
        ws[v] = jnp.where(lo, south, 0.0)
        wn[v] = jnp.where(hi, north, 0.0)
        diagonal = (west[v] + west[v + 1]) + (south + north) + SCREENING
        kk[v] = 0.8 / diagonal
        if dd is not None:
            dd[v] = diagonal


def coarsened(x, step):
    lane = lax.broadcasted_iota(jnp.int32, (8, 128), 1)
    low = (lane // step) % 2 == 0
    out = []
    for v in range(0, len(x), 2):
        y = x[v] + x[v + 1]
        out.append(0.25 * (y + jnp.where(low, lroll(y, -step), lroll(y, step))))
    return out


def pulled(x, w, level):
    wl, ws, wn = w[:3]
    step, b, a = 2**level, before(x), after(x)
    return [
        (wl[v] * b[v] + wl[v + 1] * a[v])
        + (ws[v] * lroll(x[v], step) + wn[v] * lroll(x[v], -step))
        for v in range(len(x))
    ]


def vcycle(level, rhs, start, w, coarse):
    if level == len(w):
        return coarse(rhs)
    n = len(rhs)
    kk = w[level][3]
    if start is None:
        x = [kk[v] * rhs[v] for v in range(n)]
        e = [0.2 * r + p for r, p in zip(rhs, pulled(x, w[level], level))]
    else:
        dd = w[level][4]
        p = pulled(start, w[level], level)
        x = [0.2 * start[v] + kk[v] * (rhs[v] + p[v]) for v in range(n)]
        p = pulled(x, w[level], level)
        e = [(rhs[v] - dd[v] * x[v]) + p[v] for v in range(n)]
    fix = vcycle(level + 1, coarsened(e, 2**level), None, w, coarse)
    x = [x[v] + fix[v // 2] for v in range(n)]
    p = pulled(x, w[level], level)
    return [0.2 * x[v] + kk[v] * (rhs[v] + p[v]) for v in range(n)]


def to_ring(x, sq, sq2):
    for v in range(4):
        for rep in range(4):
            sq[pl.ds(rep * 32 + v, 8, stride=4), :] = x[v]
    sq2[...] = sq[...].T
    return [sq2[pl.ds(0, 8, stride=8), :], sq2[pl.ds(64, 8, stride=8), :]]


def from_ring(x, sq, sq2, vec):
    vec[pl.ds(0, 8), :], vec[pl.ds(8, 8), :] = x[0], x[1]
    for j in range(16):
        sq[pl.ds(j * 8, 8), :] = row_of(vec, j)
    sq2[...] = sq[...].T
    return [sq2[pl.ds(v, 8, stride=4), :] for v in range(4)]


def ring_matrix(c, bmat, emat):
    sub = [lax.broadcasted_iota(jnp.int32, (8, 128), 0) + 8 * h for h in range(2)]
    half = 0.5 * 0.25**3
    east = [half * (c[h] + lroll(c[h], -1)) for h in range(2)]
    up = [pltpu.roll(c[h], 1, 0) for h in range(2)]
    dn = [pltpu.roll(c[h], 7, 0) for h in range(2)]
    first, last = sub[0] % 8 == 0, sub[0] % 8 == 7
    below = [jnp.where(first, 0.0, up[0]), jnp.where(first, up[0], up[1])]
    above = [jnp.where(last, dn[1], dn[0]), jnp.where(last, 0.0, dn[1])]
    south = [half * (c[h] + below[h]) for h in range(2)]
    north = [half * (c[h] + above[h]) for h in range(2)]
    for i in range(16):
        for h in range(2):
            j = sub[h]
            diagonal = (east[h] + lroll(east[h], 1)) + (south[h] + north[h]) + SCREENING
            value = jnp.where(j == i, diagonal, 0.0)
            value = jnp.where(j == i + 1, -south[h], value)
            value = jnp.where(j == i - 1, -north[h], value)
            bmat[pl.ds(i * 16 + h * 8, 8), :] = value
            emat[pl.ds(i * 16 + h * 8, 8), :] = jnp.where(j == i, -east[h], 0.0)


def mat(ref, i, h, base=0):
    return ref[pl.ds(base + i * 16 + h * 8, 8), :]


def matT(ref, i, h, base=0):
    return ref[pl.ds(base + h * 128 + i, 8, stride=16), :]


def inverted(a, pivots):
    sub = [lax.broadcasted_iota(jnp.int32, (8, 128), 0) + 8 * h for h in range(2)]
    for k in range(16):
        hk = k // 8
        base = k * 16
        for h in range(2):
            pivots[pl.ds(base + h * 8, 8), :] = a[k][h]
        p = 1.0 / row_of(pivots, base + k)
        scaled = [a[k][h] * p for h in range(2)]
        rk = list(scaled)
        rk[hk] = jnp.where(sub[hk] == k, 1.0 + p, rk[hk])
        new = []
        for i in range(16):
            if i == k:
                fin = list(scaled)
                fin[hk] = jnp.where(sub[hk] == k, p, fin[hk])
                new.append(fin)
                continue
            f = row_of(pivots, base + i)
            if i < k:
                f = -f
            new.append([a[i][h] - f * rk[h] for h in range(2)])
        a = new
    return a


def put(ref, a, base=0):
    for i in range(16):
        for h in range(2):
            ref[pl.ds(base + i * 16 + h * 8, 8), :] = a[i][h]


def packed_product(left, right, count):
    out = []
    for i in range(16):
        acc = [row_of(left, i * 16 + k) * right[k] for k in range(count)]
        while len(acc) > 1:
            acc = [acc[q] + acc[q + 1] for q in range(0, len(acc), 2)]
        out.append(acc[0])
    return out


def factor(bmat, emat, ps, qs, gf, left, left2, pivots):
    lane = lax.broadcasted_iota(jnp.int32, (8, 128), 1)
    group = lane // 32
    both = [(i, h) for i in range(16) for h in range(2)]
    two = range(2)

    def by_group(a, b, c, d):
        return jnp.where(group < 2, jnp.where(group == 0, a, b), jnp.where(group == 2, c, d))

    def spread(y):
        r = [y] + [lroll(y, 32 * q) for q in range(1, 4)]
        return [by_group(*(r[(g - c) % 4] for g in range(4))) for c in range(4)]

    def body(m, _):
        d = jnp.left_shift(1, m)
        base = pl.multiple_of(m * 256, 256)

        def ahead(x):
            return pltpu.roll(x, 128 - d, 1)

        def behind(x):
            return pltpu.roll(x, d, 1)

        g = inverted([[mat(bmat, i, h) for h in two] for i in range(16)], pivots)
        u = [[mat(emat, i, h) for h in two] for i in range(16)]
        ut = [[matT(emat, i, h) for h in two] for i in range(16)]
        for i, h in both:
            left[pl.ds(i * 16 + h * 8, 8), :] = jnp.where(group < 2, g[i][h], ahead(g[i][h]))
        for i in range(16):
            left2[pl.ds(i * 16, 8), :] = jnp.where(group < 2, ut[i][0], ut[i][1])
        quarters = [
            spread(y)
            for y in packed_product(left, [by_group(*u[k], *ut[k]) for k in range(16)], 16)
        ]
        q = [y[:2] for y in quarters]
        p = [y[2:] for y in quarters]
        put(ps, p, base)
        put(qs, [[behind(q[i][h]) for h in two] for i in range(16)], base)
        right = [by_group(*p[k], *(ahead(q[k][h]) for h in two)) for k in range(16)]
        first = [spread(y) for y in packed_product(emat, right, 16)]
        right = [by_group(*q[k], *q[k + 8]) for k in range(8)]
        second = []
        for y in packed_product(left2, right, 8):
            y = y + lroll(y, 64)
            z = lroll(y, 32)
            flip = group % 2 == 0
            second.append([jnp.where(flip, y, z), jnp.where(flip, z, y)])
        for i, h in both:
            rows_at = pl.ds(i * 16 + h * 8, 8)
            bmat[rows_at, :] = bmat[rows_at, :] - (first[i][h] + behind(second[i][h]))
            emat[rows_at, :] = -first[i][2 + h]
        return 0

    lax.fori_loop(0, 5, body, 0)
    last = [[mat(bmat, i, h) + (mat(emat, i, h) + matT(emat, i, h)) for h in two] for i in range(16)]
    put(gf, inverted(last, pivots))


def times(ref, base, vec, x):
    vec[pl.ds(0, 8), :], vec[pl.ds(8, 8), :] = x[0], x[1]
    out = []
    for h in range(2):
        terms = [mat(ref, k, h, base) * row_of(vec, k) for k in range(16)]
        while len(terms) > 1:
            terms = [terms[q] + terms[q + 1] for q in range(0, len(terms), 2)]
        out.append(terms[0])
    return out


def ring_solve(r, ps, qs, gf, vecs):
    for m in range(5):
        d = 1 << m
        p = times(ps, m * 256, vecs.at[2 * m], [lroll(r[h], -d) for h in range(2)])
        q = times(qs, m * 256, vecs.at[2 * m + 1], [lroll(r[h], d) for h in range(2)])
        r = [r[h] - (p[h] + q[h]) for h in range(2)]
    return times(gf, 0, vecs.at[10], r)


def coarse_setup(coarse, ring, mats):
    sq, sq2, vecs = ring
    bmat, emat, ps, qs, gf, left, left2, pivots = mats
    lane = lax.broadcasted_iota(jnp.int32, (8, 128), 1)
    for v in range(4):
        y = coarse[pl.ds(v * 8, 8), :] * (SCALE / 64.0)
        for step in (1, 2, 4):
            y = y + jnp.where((lane // step) % 2 == 0, lroll(y, -step), lroll(y, step))
        for rep in range(4):
            sq[pl.ds(rep * 32 + v * 8, 8), :] = y
    sq2[...] = sq[...].T
    ring_matrix([sq2[pl.ds(64 * h, 8, stride=8), :] for h in range(2)], bmat, emat)
    factor(bmat, emat, ps, qs, gf, left, left2, pivots)


def conductance_setup(gath, w):
    cond = [gath[0, pl.ds(v, 8, stride=NV), :] * SCALE for v in range(NV)]
    level_weights(cond, 0, *w[0])
    c = coarsened(cond, 1)
    level_weights(c, 1, *w[1])
    level_weights(coarsened(c, 2), 2, *w[2])


def cycles(gath, w, ring, mats, pot):
    sq, sq2, vecs = ring
    ps, qs, gf = mats[2:5]

    def coarse(r):
        x = ring_solve(to_ring(r, sq, sq2), ps, qs, gf, vecs)
        return from_ring(x, sq, sq2, vecs.at[11])

    def sweep(start):
        source = [gath[1, pl.ds(v, 8, stride=NV), :] * SCALE for v in range(NV)]
        x = vcycle(0, source, start, w, coarse)
        for v in range(NV):
            pot[v] = x[v]

    def body(_, carry):
        sweep([pot[v] for v in range(NV)])
        return carry

    sweep(None)
    lax.fori_loop(1, CYCLES, body, 0)


def stencil(pot, west, east):
    lane = lax.broadcasted_iota(jnp.int32, (8, 128), 1)
    low, high = lane == 0, lane == 127

    def slope(q):
        return jnp.where(high, 0.0, lroll(q, -1)) - jnp.where(low, 0.0, lroll(q, 1))

    uw = CAP * jnp.tanh(-0.25 * slope(west + pot))
    ue = CAP * jnp.tanh(-0.25 * slope(pot + east))
    r = east - west
    us = jnp.where(low, 0.0, CAP * jnp.tanh(0.25 * (lroll(r, 1) + r)))
    un = jnp.where(high, 0.0, lroll(us, -1))
    pos = [jnp.maximum(u, 0.0) for u in (uw, ue, us, un)]
    neg = [jnp.minimum(u, 0.0) for u in (uw, ue, us, un)]
    centre = 1.0 - (pos[1] - neg[0]) - (pos[3] - neg[2])
    return centre, pos[0], -neg[1], pos[2], -neg[3]


def dynamo_kernel(
    nt, nl, ped_hbm, wind_hbm, cour_hbm, dens_hbm,
    coef, pot_own, ent, sides, dens, halo, atab, btab,
    ped, wind, cour, part, parts, gath, crow, crows, coarse, rows32, bsend, brecv, psend,
    wl0, ws0, wn0, kk0, dd0, wl1, ws1, wn1, kk1, wl2, ws2, wn2, kk2,
    sq, sq2, bmat, emat, ps, qs, gf, left, left2, pivots, vecs, pot, whole,
    s_ld, s_t, r_t, s_l, r_l, s_h, r_h, s_b, r_b, s_p, r_p, s_e, r_e, s_c, r_c, line,
):
    ns, pts = dens.shape[:2]
    t, l = lax.axis_index("tube"), lax.axis_index("lon")
    loads = [
        pltpu.make_async_copy(src, dst, s_ld.at[k])
        for k, (src, dst) in enumerate(
            ((ped_hbm, ped), (wind_hbm, wind), (cour_hbm, cour), (dens_hbm, dens))
        )
    ]
    for c in loads:
        c.start()

    far_t = sorted(range(1, nt), key=lambda o: -min(o, nt - o))
    far_l = sorted(range(1, nl), key=lambda o: -min(o // 2 % 4, 4 - o // 2 % 4) - min(o // 8, 4 - o // 8))
    beside = l + 1 - 2 * lax.rem(l, 2)
    x_line = [l - lax.rem(l, 8) + lax.rem(lax.rem(l, 8) + 2 * o, 8) for o in range(1, 4)]
    y_line = [lax.rem(c + 8 * o, nl) for c in (l, beside) for o in range(1, nl // 8)]
    next_chip = lax.rem(l + 2 * lax.rem(l, 2) - 1 + nl, nl)
    across_lon = y_line + x_line + [beside, next_chip]
    greeted = [(t, c) for c in across_lon] + [(lax.rem(t + o, nt), l) for o in far_t]
    barrier = pltpu.get_barrier_semaphore()
    for to in greeted:
        pl.semaphore_signal(barrier, inc=1, device_id=to, device_id_type=MESH)

    def summed(terms):
        terms = list(terms)
        while len(terms) > 1:
            terms = [x + y for x, y in zip(terms[::2], terms[1::2])] + terms[len(terms) & ~1 :]
        return terms[0]

    loads[0].wait()
    part[0] = total = summed(ped[p] for p in range(pts))
    crow[...] = jnp.sum(total, axis=0, keepdims=True)

    def remote(src, dst, ssem, rsem, to):
        c = pltpu.make_async_remote_copy(
            src_ref=src, dst_ref=dst, send_sem=ssem, recv_sem=rsem,
            device_id=to, device_id_type=MESH,
        )
        c.start()
        return c

    def settle(ref, sem):
        pltpu.make_async_copy(ref, ref, sem).wait()

    pl.semaphore_wait(barrier, len(greeted))
    for o in far_t:
        to = (lax.rem(t + o, nt), l)
        remote(crow, crows.at[o], s_c.at[0], r_c.at[0], to)
    for c in x_line:
        pl.semaphore_signal(line, inc=1, device_id=(t, c), device_id_type=MESH)
    fields = [pl.ds(k * (2 // SPLIT), 2 // SPLIT) for k in range(SPLIT)]
    for k in range(SPLIT):
        if k == SPLIT - 1:
            loads[1].wait()
            part[1] = summed(ped[p] * wind[p] for p in range(pts))
        for o in far_t:
            to = (lax.rem(t + o, nt), l)
            remote(part.at[fields[k]], parts.at[o, fields[k]], s_t.at[k], r_t.at[k], to)

    right, left_l = lax.rem(l + 1, nl), lax.rem(l + nl - 1, nl)
    h0 = remote(
        dens_hbm.at[:, :, pl.ds(7, 1), :], halo.at[:, :, pl.ds(0, 1), :], s_h.at[0], r_h.at[0], (t, right)
    )
    h1 = remote(
        dens_hbm.at[:, :, pl.ds(0, 1), :], halo.at[:, :, pl.ds(7, 1), :], s_h.at[1], r_h.at[1], (t, left_l)
    )

    loads[2].wait()
    coefficient_tables(cour, atab, btab)
    loads[3].wait()

    def step(p, carry):
        out = []
        for s in range(ns):
            x, m = carry[s]
            a, b = row_of(atab, p * 8 + s), row_of(btab, p * 8 + s)
            out.append((a * x + b * dens[s, p], a * m))
        return tuple(out)

    zero, one = jnp.zeros((8, 128), F32), jnp.ones((8, 128), F32)
    ends = lax.fori_loop(0, pts, step, tuple((zero, one) for _ in range(ns)))
    for s in range(ns):
        bsend[s, 0] = ends[s][0]
        bsend[s, 1] = ends[s][1]

    mine = (t * ns + nt - 1) // nt
    owner_of = [(s * nt) // ns for s in range(ns)]
    is_owner = jnp.logical_and(mine < ns, (mine * nt) // ns == t)
    for s in range(ns):

        @pl.when(t != owner_of[s])
        def _():
            o = lax.rem(t - owner_of[s] + nt, nt)
            remote(bsend.at[s], brecv.at[o], s_b, r_b, (owner_of[s], l))

    others_t, others_l = pl.ds(1, nt - 1), pl.ds(0, (nl - 1) * 8)
    settle(crows.at[others_t], r_c.at[0])
    total = [crow[...]] + [crows[o] for o in range(1, nt)]
    while len(total) > 1:
        total = [total[q] + total[q + 1] for q in range(0, len(total), 2)]
    coarse[l] = total[0]
    pl.semaphore_wait(line, len(x_line))
    for o in far_l:
        to = (t, lax.rem(l + o, nl))
        remote(coarse.at[l], coarse.at[l], s_c.at[1], r_c.at[1], to)
    block = pl.ds(pl.multiple_of(l * 8, 8), 8)
    for k in range(SPLIT):
        settle(parts.at[others_t, fields[k]], r_t.at[k])
        total = [part[fields[k]]] + [parts[o, fields[k]] for o in range(1, nt)]
        while len(total) > 1:
            total = [total[q] + total[q + 1] for q in range(0, len(total), 2)]
        gath[fields[k], block, :] = total[0]
        for o in far_l:
            to = (t, lax.rem(l + o, nl))
            at = gath.at[fields[k], block, :]
            remote(at, at, s_l.at[k], r_l.at[k], to)

    west_row, east_row = pl.ds(0, 1), pl.ds(7, 1)

    @pl.when(is_owner)
    def _():
        brecv[0] = bsend[mine]
        settle(brecv.at[others_t], r_b)
        x = zero
        for k in range(nt):
            psend[k] = x
            o = lax.rem(k - t + nt, nt)
            x = brecv[o, 1] * x + brecv[o, 0]
        ent[mine] = psend[t]
        for o in far_t + [0]:
            to = lax.rem(t + o, nt)
            if o:
                remote(psend.at[to], ent.at[mine], s_p, r_p, (to, l))
            for k, (row, side) in enumerate(((east_row, right), (west_row, left_l))):
                remote(psend.at[to, row], sides.at[mine, west_row if k == 0 else east_row],
                       s_e, r_e, (to, side))

    w = [(wl0, ws0, wn0, kk0, dd0), (wl1, ws1, wn1, kk1, None), (wl2, ws2, wn2, kk2, None)]
    ring, mats = (sq, sq2, vecs), (bmat, emat, ps, qs, gf, left, left2, pivots)
    settle(crows.at[others_t], s_c.at[0])
    for k in range(SPLIT):
        settle(parts.at[others_t, fields[k]], s_t.at[k])
    for c in (h0, h1):
        c.wait()
    settle(coarse.at[pl.ds(0, nl - 1)], r_c.at[1])
    for r in range(nl):
        rows32[pl.ds(r, 1), :] = coarse[r]
    coarse_setup(rows32, ring, mats)
    settle(gath.at[fields[0], others_l], r_l.at[0])
    conductance_setup(gath, w)

    for k in range(1, SPLIT):
        settle(gath.at[fields[k], others_l], r_l.at[k])
    cycles(gath, w, ring, mats, pot)
    for v in range(NV):
        whole[pl.ds(v, 8, stride=NV), :] = pot[v]
    own = whole[pl.ds(pl.multiple_of(l * 8, 8), 8), :]
    sub = lax.broadcasted_iota(jnp.int32, (8, 128), 0)
    west = jnp.where(sub == 0, row_of(whole, lax.rem(l * 8 + 255, 256)), pltpu.roll(own, 1, 0))
    east = jnp.where(sub == 7, row_of(whole, lax.rem(l * 8 + 8, 256)), pltpu.roll(own, 7, 0))
    pot_own[...] = own
    for k, c in enumerate(stencil(own, west, east)):
        coef[k] = c

    settle(coarse.at[pl.ds(0, nl - 1)], s_c.at[1])
    for k in range(SPLIT):
        settle(gath.at[fields[k], others_l], s_l.at[k])

    @pl.when(is_owner)
    def _():
        settle(bsend.at[pl.ds(0, ns - 1)], s_b)
        settle(ent.at[pl.ds(0, ns - 1)], r_p)
        settle(psend.at[others_t], s_p)
        settle(psend.at[pl.ds(0, nt // 4)], s_e)

    @pl.when(jnp.logical_not(is_owner))
    def _():
        settle(bsend, s_b)
        settle(ent, r_p)

    settle(sides.at[:, pl.ds(0, 2), :], r_e)


VM = pl.BlockSpec(memory_space=pltpu.VMEM)
HBM = pl.BlockSpec(memory_space=pltpu.HBM)


def tiles(*n):
    return pltpu.VMEM((*n, 8, 128), F32)


def rows(n):
    return pltpu.VMEM((n, 128), F32)


def dynamo(mesh, density, pedersen, wind, courant):
    nt, nl = mesh.shape["tube"], mesh.shape["lon"]
    ns, pts = density.shape[:2]
    dma = pltpu.SemaphoreType.DMA
    state = jax.ShapeDtypeStruct((ns, 8, 128), F32)
    table = jax.ShapeDtypeStruct((pts * 8, 128), F32)
    levels = [tiles(33)] + [tiles(32)] * 4 + [tiles(17)] + [tiles(16)] * 3 + [tiles(9)] + [tiles(8)] * 3
    return pl.pallas_call(
        functools.partial(dynamo_kernel, nt, nl),
        out_shape=(
            jax.ShapeDtypeStruct((5, 8, 128), F32),
            jax.ShapeDtypeStruct((8, 128), F32),
            state, state,
            jax.ShapeDtypeStruct(density.shape, F32),
            jax.ShapeDtypeStruct(density.shape, F32),
            table, table,
        ),
        in_specs=[HBM] * 4,
        out_specs=(VM,) * 8,
        scratch_shapes=[
            tiles(pts), tiles(pts), pltpu.VMEM((ns, pts), F32),
            tiles(2), tiles(nt, 2), pltpu.VMEM((2, 8 * nl, 128), F32),
            rows(1), pltpu.VMEM((nt, 1, 128), F32), pltpu.VMEM((nl, 1, 128), F32), rows(nl),
            tiles(ns, 2), tiles(nt, 2), tiles(nt),
        ]
        + levels
        + [rows(128), rows(128), rows(256), rows(256), rows(5 * 256), rows(5 * 256), rows(256)]
        + [rows(256), rows(256), rows(256), pltpu.VMEM((12, 16, 128), F32), tiles(NV), rows(256)]
        + [
            dma((4,)), dma((2,)), dma((2,)), dma((2,)), dma((2,)), dma((2,)), dma((2,)),
            dma, dma, dma, dma, dma, dma, dma((2,)), dma((2,)), pltpu.SemaphoreType.REGULAR,
        ],
        compiler_params=pltpu.CompilerParams(
            collective_id=0, has_side_effects=True, vmem_limit_bytes=40 * 2**20
        ),
        name="dynamo",
    )(pedersen, wind, courant, density)


def transport_kernel(coef, pot_in, ent, sides, dens, halo, atab, btab, out_hbm, pot, out, sem):
    ns, pts = out.shape[:2]
    pot[...] = pot_in[...]
    cc, cw, ce, cs, cn = (coef[k] for k in range(5))
    sub = lax.broadcasted_iota(jnp.int32, (8, 128), 0)
    start = [(ent[s], sides[s]) for s in range(ns)]

    def step(p, carry):
        new = []
        for s in range(ns):
            y, side = carry[s]
            a, b = row_of(atab, p * 8 + s), row_of(btab, p * 8 + s)
            y = a * y + b * dens[s, p]
            side = a * side + b * halo[s, p]
            yw = jnp.where(sub == 0, side, pltpu.roll(y, 1, 0))
            ye = jnp.where(sub == 7, side, pltpu.roll(y, 7, 0))
            out[s, p] = (cc * y + (cw * yw + ce * ye)) + (cs * lroll(y, 1) + cn * lroll(y, -1))
            new.append((y, side))
        return tuple(new)

    stores, carry = [], tuple(start)
    for k in range(pts // CHUNK):
        carry = lax.fori_loop(k * CHUNK, (k + 1) * CHUNK, step, carry, unroll=True)
        at = pl.ds(k * CHUNK, CHUNK)
        stores.append(pltpu.make_async_copy(out.at[:, at], out_hbm.at[:, at], sem.at[k]))
        stores[-1].start()
    for c in stores:
        c.wait()


def transport(coef, pot, ent, sides, density, halo, atab, btab):
    return pl.pallas_call(
        transport_kernel,
        out_shape=(
            jax.ShapeDtypeStruct(density.shape, F32),
            jax.ShapeDtypeStruct((8, 128), F32),
        ),
        in_specs=[VM] * 8,
        out_specs=(pl.BlockSpec(memory_space=pl.ANY), VM),
        scratch_shapes=[pltpu.VMEM(density.shape, F32), pltpu.SemaphoreType.DMA((density.shape[1] // CHUNK,))],
        compiler_params=pltpu.CompilerParams(vmem_limit_bytes=24 * 2**20),
        name="transport",
    )(coef, pot, ent, sides, density, halo, atab, btab)


def solution(mesh):
    def on_device(density, pedersen, wind, courant):
        args = (density, pedersen, wind, courant)
        args = (pltpu.with_memory_space_constraint(x, pltpu.HBM) for x in args)
        return transport(*dynamo(mesh, *args))

    return jax.shard_map(
        on_device,
        mesh=mesh,
        in_specs=(
            P(None, "tube", "lon", None),
            P("tube", "lon", None),
            P("tube", "lon", None),
            P(None, "tube"),
        ),
        out_specs=(P(None, "tube", "lon", None), P("lon", None)),
        check_vma=False,
    )
```
